256 devices in a mesh: seq: 32 (over y, z), head: 8 (over x, core).
Axes of the slice: x: 4, y: 4, z: 8, core: 2. Of those that a mesh axis runs over, the one named last changes fastest.
Arguments:
- queries: bfloat16 [32768, 1024], P('seq', 'head'), may hold values from -25 to 25
- keys: bfloat16 [32768, 1024], P('seq', 'head'), may hold values from -6 to 6
- values: bfloat16 [32768, 1024], P('seq', 'head'), may hold values from -6 to 6
- grad_out: bfloat16 [32768, 1024], P('seq', 'head'), may hold values from -192 to 192
- out_weight: bfloat16 [1024, 1024], P('head'), may hold values from -0.1875 to 0.1875
- random_blocks: int32 [256, 3], replicated, may hold values from 0 to 255, as said below
- global_blocks: int32 [2], replicated, may hold values from 0 to 255
Outputs:
- grad_queries: float32 [32768, 1024], P('seq', 'head')
- grad_keys: float32 [32768, 1024], P('seq', 'head')
- grad_values: float32 [32768, 1024], P('seq', 'head')
The draws below stay inside these ranges and needn't reach their ends.
Inputs may be any that keep to these rules, and one draw needn't show every extreme that they name: `random_blocks`: cut the rows into aligned runs of 8 rows. Within one run, at most 2 of its 24 entries share one value of entry // 8, and in every run some value of entry // 8 is shared by exactly 2 entries.
All inputs are finite; a program needn't handle non-finite values.
Results may differ from the reference program's by a relative error of at most 0.0083.
Values may be sent and summed in bfloat16 or wider, within the bound.
No kernel may reach another device: no remote copies, remote signals or barrier semaphores. Data moves between devices by JAX's collectives and lax.ppermute only.
A program may use at most 128 MiB of HBM per device.

```python
import math
import jax
import jax.numpy as jnp
from jax import lax

HEADS = 8
HEAD_FEATURES = 128
BLOCK_TOKENS = 128
GLOBALS = 2
RANDOMS = 3
QUERY_BLOCKS_PER = 8
WIDTH = 1024
BLOCKS = 256
TOKENS = 32768
CAP = 2
N_SEQ = 32


def draw_queries(key, part):
    key = jax.random.fold_in(key, 3)
    return jnp.clip(jax.random.normal(key, (TOKENS, WIDTH), jnp.float32), -6.0, 6.0).astype(jnp.bfloat16)


def draw_keys(key, part):
    key = jax.random.fold_in(key, 5)
    return jnp.clip(jax.random.normal(key, (TOKENS, WIDTH), jnp.float32), -6.0, 6.0).astype(jnp.bfloat16)


def draw_random_blocks(key, part):
    key = jax.random.fold_in(key, 7)
    pair_count = QUERY_BLOCKS_PER * RANDOMS

    def one_run(run_key):
        order = jax.random.permutation(jax.random.fold_in(run_key, 1), pair_count)
        owners = jax.random.permutation(jax.random.fold_in(run_key, 2), N_SEQ)
        local_ids = jax.random.randint(jax.random.fold_in(run_key, 3), (pair_count,), 0, QUERY_BLOCKS_PER)
        return owners[order // CAP] * QUERY_BLOCKS_PER + local_ids
    drawn = jax.vmap(one_run)(jax.random.split(key, N_SEQ))
    return drawn.reshape(BLOCKS, RANDOMS).astype(jnp.int32)


def shard_levels(own_key, shape, cuts, low, largest):
    gain, own = 1.0, jax.random.fold_in(own_key, 6)
    for position, parts in cuts:
        draws = jnp.exp(jax.random.uniform(jax.random.fold_in(own, position), (parts,), jnp.float32, low / len(cuts), largest / len(cuts)))
        gain = gain * jnp.repeat(draws, shape[position] // parts).reshape([-1 if axis == position else 1 for axis in range(len(shape))])
    return gain


def bell_draw(stream_key, shape, deviation, limit, shards=(), kind=jnp.bfloat16):
    loudness = shard_levels(stream_key, shape, shards, -0.22, 0.18) if shards else 1.0
    result = jax.random.normal(stream_key, shape, jnp.float32) * deviation * loudness
    return jnp.minimum(jnp.maximum(result, -limit), limit).astype(kind)


def setup_inputs(seed: int = 0) -> dict:
    seeds = jax.random.split(jax.random.key(seed), 8)
    queries = draw_queries(jax.random.fold_in(seeds[7], 71), 0)
    keys = draw_keys(jax.random.fold_in(seeds[7], 71), 0)
    values = bell_draw(seeds[2], (TOKENS, WIDTH), 1.0, 6.0, ((0, 32), (1, 8)))
    grad_out = bell_draw(seeds[3], (TOKENS, WIDTH), 32.0, 192.0, ((0, 32), (1, 8)))
    out_weight = bell_draw(seeds[4], (WIDTH, WIDTH), WIDTH ** -0.5, 0.1875, ((0, 8),))
    random_blocks = draw_random_blocks(jax.random.fold_in(seeds[7], 71), 0)
    global_blocks = jax.random.randint(seeds[6], (GLOBALS,), 0, BLOCKS).astype(jnp.int32)
    return dict(queries=queries, keys=keys, values=values, grad_out=grad_out, out_weight=out_weight, random_blocks=random_blocks, global_blocks=global_blocks)


def rounded(values_f32):
    return lax.optimization_barrier(values_f32.astype(jnp.bfloat16)).astype(jnp.float32)

def block_lists(random_blocks, global_blocks):
    block_ids = jnp.arange(BLOCKS, dtype=jnp.int32)
    key_lists = jnp.concatenate([jnp.stack([block_ids - 1, block_ids, block_ids + 1], axis=1), jnp.broadcast_to(global_blocks.astype(jnp.int32)[None, :], (BLOCKS, GLOBALS)), random_blocks.astype(jnp.int32)], axis=1).astype(jnp.int32)
    slot_valid = jnp.concatenate([(block_ids >= 1)[:, None], jnp.ones((BLOCKS, 1), bool), (block_ids + 1 < BLOCKS)[:, None], jnp.ones((BLOCKS, GLOBALS + RANDOMS), bool)], axis=1)
    return (jnp.clip(key_lists, 0, BLOCKS - 1).astype(jnp.int32), slot_valid)

def one_head(query_head, key_head, value_head, upstream_head, key_lists, slot_valid):
    count_of_slots = 3 + GLOBALS + RANDOMS
    logit_scale = 1.0 / math.sqrt(HEAD_FEATURES)
    key_blocks = key_head.reshape(BLOCKS, BLOCK_TOKENS, HEAD_FEATURES)
    value_blocks = value_head.reshape(BLOCKS, BLOCK_TOKENS, HEAD_FEATURES)
    query_blocks = query_head.reshape(BLOCKS, BLOCK_TOKENS, HEAD_FEATURES)
    upstream_blocks = upstream_head.reshape(BLOCKS, BLOCK_TOKENS, HEAD_FEATURES)

    def group_step(totals, group_index):
        grad_key_all, grad_value_all = totals
        first_block = (group_index * QUERY_BLOCKS_PER).astype(jnp.int32)
        chosen = lax.dynamic_slice_in_dim(key_lists, first_block, QUERY_BLOCKS_PER, 0)
        allowed = lax.dynamic_slice_in_dim(slot_valid, first_block, QUERY_BLOCKS_PER, 0)
        key_matrix = key_blocks[chosen].reshape(QUERY_BLOCKS_PER, count_of_slots * BLOCK_TOKENS, HEAD_FEATURES).astype(jnp.float32)
        value_matrix = value_blocks[chosen].reshape(QUERY_BLOCKS_PER, count_of_slots * BLOCK_TOKENS, HEAD_FEATURES).astype(jnp.float32)
        query_matrix = lax.dynamic_slice_in_dim(query_blocks, first_block, QUERY_BLOCKS_PER, 0).astype(jnp.float32)
        incoming_gradient_rows = lax.dynamic_slice_in_dim(upstream_blocks, first_block, QUERY_BLOCKS_PER, 0).astype(jnp.float32)
        key_valid = jnp.repeat(allowed, BLOCK_TOKENS, axis=1)[:, None, :]
        attention_logits = jnp.einsum('vhg,vrg->vhr', query_matrix, key_matrix) * logit_scale
        attention_logits = jnp.where(key_valid, attention_logits, -1e+30)
        row_max = lax.optimization_barrier(jnp.max(attention_logits, axis=-1, keepdims=True))
        weights = jnp.where(key_valid, jnp.exp(attention_logits - row_max), 0.0)
        probs = weights / lax.optimization_barrier(jnp.sum(weights, axis=-1, keepdims=True))
        probabilities_reduced = probs.astype(jnp.bfloat16).astype(jnp.float32)
        attended_output = jnp.einsum('myz,mzj->myj', probabilities_reduced, value_matrix)
        row_delta = lax.optimization_barrier(jnp.sum(incoming_gradient_rows * attended_output, axis=-1))
        probability_gradient = jnp.einsum('vhg,vrg->vhr', incoming_gradient_rows, value_matrix)
        score_gradient = (probs * (probability_gradient - row_delta[..., None]) * logit_scale).astype(jnp.bfloat16).astype(jnp.float32)
        query_gradient = jnp.einsum('myz,mzj->myj', score_gradient, key_matrix)
        key_gradient = jnp.einsum('ipe,ipn->ien', score_gradient, query_matrix).reshape(QUERY_BLOCKS_PER, count_of_slots, BLOCK_TOKENS, HEAD_FEATURES)
        value_gradient = jnp.einsum('ipe,ipn->ien', probabilities_reduced, incoming_gradient_rows).reshape(QUERY_BLOCKS_PER, count_of_slots, BLOCK_TOKENS, HEAD_FEATURES)
        window_ids = chosen[:, :3]
        random_ids = chosen[:, 3 + GLOBALS:]
        global_ids = chosen[0, 3:3 + GLOBALS]
        grad_key_all = grad_key_all.at[window_ids].add(key_gradient[:, :3])
        grad_value_all = grad_value_all.at[window_ids].add(value_gradient[:, :3])
        grad_key_all = grad_key_all.at[random_ids].add(rounded(key_gradient[:, 3 + GLOBALS:]))
        grad_value_all = grad_value_all.at[random_ids].add(rounded(value_gradient[:, 3 + GLOBALS:]))
        grad_key_all = grad_key_all.at[global_ids].add(rounded(lax.optimization_barrier(jnp.sum(key_gradient[:, 3:3 + GLOBALS], axis=0))))
        grad_value_all = grad_value_all.at[global_ids].add(rounded(lax.optimization_barrier(jnp.sum(value_gradient[:, 3:3 + GLOBALS], axis=0))))
        return ((grad_key_all, grad_value_all), query_gradient)
    empty = jnp.zeros((BLOCKS, BLOCK_TOKENS, HEAD_FEATURES), jnp.float32)
    (grad_key_all, grad_value_all), query_gradient = lax.scan(group_step, (empty, empty), jnp.arange(N_SEQ, dtype=jnp.int32))
    return (query_gradient.reshape(TOKENS, HEAD_FEATURES), grad_key_all.reshape(TOKENS, HEAD_FEATURES), grad_value_all.reshape(TOKENS, HEAD_FEATURES))

def reference(queries, keys, values, grad_out, out_weight, random_blocks, global_blocks):
    upstream = jnp.dot(grad_out, out_weight.T, preferred_element_type=jnp.float32).astype(jnp.bfloat16)
    key_lists, slot_valid = block_lists(random_blocks, global_blocks)

    def per_head(arrays):
        return one_head(arrays[0], arrays[1], arrays[2], arrays[3], key_lists, slot_valid)

    def split_heads(array):
        return array.reshape(TOKENS, HEADS, HEAD_FEATURES).transpose(1, 0, 2)
    query_gradient, key_gradient, value_gradient = lax.map(per_head, (split_heads(queries), split_heads(keys), split_heads(values), split_heads(upstream)))

    def join_heads(array):
        return array.transpose(1, 0, 2).reshape(TOKENS, WIDTH)
    return (join_heads(query_gradient), join_heads(key_gradient), join_heads(value_gradient))
```

```python
import math

import jax
import jax.numpy as jnp
from jax import lax
from jax.experimental import pallas as pl
from jax.experimental.pallas import tpu as pltpu
from jax.sharding import PartitionSpec as P

T = 128
GLOBALS = 2
RANDOMS = 3
NB = 8
NY = 4
NZ = 8
RAND = NB * RANDOMS
REQ = RAND + GLOBALS
ROWBLK = NZ * NB
FIN = 18
REL = 9

RU, RD = 0, REL
FU, FD = 2 * REL, 2 * REL + FIN
ME = 2 * REL + 2 * FIN
PLAN = ME + REQ + 2

BF = jnp.bfloat16
F32 = jnp.float32
VMEM = pl.BlockSpec(memory_space=pltpu.VMEM)
SMEM = pl.BlockSpec(memory_space=pltpu.SMEM)


def call(kernel, outs, ins, scratch=(), smem_out=False, aliases=None, flops=0, moved=0, limit=48):
    return pl.pallas_call(
        kernel,
        out_shape=outs,
        in_specs=ins,
        out_specs=jax.tree.map(lambda _: SMEM if smem_out else VMEM, outs),
        scratch_shapes=list(scratch),
        input_output_aliases=aliases or {},
        cost_estimate=pl.CostEstimate(flops=flops, bytes_accessed=moved, transcendentals=0),
        compiler_params=pltpu.CompilerParams(vmem_limit_bytes=limit * 1024 * 1024),
    )


def blocks(n, dtype=BF):
    return jax.ShapeDtypeStruct((n, T, T), dtype)


def plan_kernel(tab, plan):
    y, z = tab[NY * REQ], tab[NY * REQ + 1]

    def clear(j, c):
        plan[j] = -1
        return c

    lax.fori_loop(0, ME, clear, 0)
    plan[ME + REQ] = y
    plan[ME + REQ + 1] = z
    for off in range(NY):
        yd = (y + off) & (NY - 1)

        def where(k):
            b = tab[yd * REQ + k]
            far = ((b >> 6) - yd) & (NY - 1)
            return far, ((((b >> 3) - z) & (NZ - 1)) << 3) | (b & 7)

        def count(k, c):
            far, _ = where(k)
            return tuple(n + (far == r).astype(jnp.int32) for n, r in zip(c, (1, 2, 3)))

        zero = jnp.int32(0)
        ahead, across, behind = lax.fori_loop(0, REQ, count, (zero, zero, zero))
        low = jnp.maximum(jnp.maximum(across - REL, ahead + across - FIN), 0)
        high = jnp.minimum(jnp.minimum(across, REL), FIN - behind)
        via = jnp.minimum(jnp.maximum(across >> 1, low), high)

        def place(k, c):
            used_ahead, used_across, used_behind = c
            far, src = where(k)
            is1, is2, is3 = far == 1, far == 2, far == 3
            first = used_across < via
            down_slot = jnp.where(is3, used_behind, behind + used_across)
            up_slot = jnp.where(is1, used_ahead, ahead + used_across - via)
            from_behind = is3 | (is2 & first)
            from_ahead = is1 | (is2 & jnp.logical_not(first))
            if off == 0:
                plan[ME + k] = jnp.where(
                    from_behind,
                    ROWBLK + down_slot,
                    jnp.where(from_ahead, ROWBLK + FIN + up_slot, src),
                )
            elif off == 1:

                @pl.when(from_behind)
                def _():
                    plan[FU + down_slot] = jnp.where(is3, src, ROWBLK + used_across)
            elif off == 3:

                @pl.when(from_ahead)
                def _():
                    plan[FD + up_slot] = jnp.where(is1, src, ROWBLK + used_across - via)
            else:

                @pl.when(is2)
                def _():
                    plan[jnp.where(first, RU + used_across, RD + used_across - via)] = src

            return (
                used_ahead + is1.astype(jnp.int32),
                used_across + is2.astype(jnp.int32),
                used_behind + is3.astype(jnp.int32),
            )

        lax.fori_loop(0, REQ, place, (zero, zero, zero))


def loop(n, body):
    def step(j, c):
        body(j)
        return c

    lax.fori_loop(0, n, step, 0)


def from_row(src, pieces, put):
    for r, piece in enumerate(pieces):

        @pl.when((src >> 3) == r)
        def _():
            put(piece[src & 7])


def pack_kernel(plan, *refs):
    pieces, (ru, rd, fu, fd) = refs[:NZ], refs[NZ:]
    for base, n, out in ((RU, REL, ru), (RD, REL, rd), (FU, FIN, fu), (FD, FIN, fd)):

        def one(j):
            def put(v):
                out[j] = v

            from_row(plan[base + j], pieces, put)

        loop(n, one)


def relay_kernel(plan, got_up, got_down, fu_in, fd_in, fu, fd):
    for base, got, into, out in ((FU, got_up, fu_in, fu), (FD, got_down, fd_in, fd)):

        def one(j):
            src = plan[base + j]

            @pl.when(src >= ROWBLK)
            def _():
                out[j] = got[src - ROWBLK]

            @pl.when(src < ROWBLK)
            def _():
                out[j] = into[j]

        loop(FIN, one)


def attention_kernel(plan, q, u, *refs):
    kp, vp = refs[:NZ], refs[NZ : 2 * NZ]
    below, above, kb, ka, vb, va = refs[2 * NZ : 2 * NZ + 6]
    dq, gk, gv, eb, ea, rkb, rka, rvb, rva, lk, lv = refs[2 * NZ + 6 : 2 * NZ + 17]
    kall, vall, ak, av, sk, sv = refs[2 * NZ + 17 :]
    at = plan[ME + REQ] * NZ + plan[ME + REQ + 1]
    for which, (full, pieces, behind, ahead) in enumerate(((kall, kp, kb, ka), (vall, vp, vb, va))):
        full[0] = below[which]
        full[pl.ds(1, NB)] = pieces[0][...]
        full[NB + 1] = above[which]

        def one(k):
            src = plan[ME + k]

            def put(v):
                full[NB + 2 + k] = v

            from_row(src, pieces, put)

            @pl.when((src >= ROWBLK) & (src < ROWBLK + FIN))
            def _():
                put(behind[src - ROWBLK])

            @pl.when(src >= ROWBLK + FIN)
            def _():
                put(ahead[src - ROWBLK - FIN])

        loop(REQ, one)
    ak[...] = jnp.zeros_like(ak)
    av[...] = jnp.zeros_like(av)
    sk[...] = jnp.zeros_like(sk)
    sv[...] = jnp.zeros_like(sv)
    scale = 1.0 / math.sqrt(T)
    nt = (((1,), (1,)), ((), ()))
    tn = (((0,), (0,)), ((), ()))

    def block(i):
        qi, ui = q[i], u[i]
        spans = (
            (pl.ds(i, 3), 3),
            (pl.ds(NB + 2 + RAND, GLOBALS), GLOBALS),
            (pl.ds(NB + 2 + RANDOMS * i, RANDOMS), RANDOMS),
        )
        keys = [kall[s].reshape(n * T, T) for s, n in spans]
        vals = [vall[s].reshape(n * T, T) for s, n in spans]
        no_below = jnp.where((at == 0) & (i == 0), -1e30, 0.0)
        no_above = jnp.where((at == NY * NZ - 1) & (i == NB - 1), -1e30, 0.0)
        logits = [
            lax.dot_general(k, qi, nt, preferred_element_type=F32) * (scale * math.log2(math.e))
            for k in keys
        ]
        window = logits[0]
        logits[0] = jnp.concatenate(
            [window[:T] + no_below, window[T : 2 * T], window[2 * T :] + no_above], axis=0
        )
        top = logits[0].max(axis=0, keepdims=True)
        for x in logits[1:]:
            top = jnp.maximum(top, x.max(axis=0, keepdims=True))
        weights = [jnp.exp2(x - top) for x in logits]
        total = sum(w.sum(axis=0, keepdims=True) for w in weights)
        inverse = 1.0 / total
        probs = [w * inverse for w in weights]
        low = [p.astype(BF) for p in probs]
        gp = [lax.dot_general(v, ui, nt, preferred_element_type=F32) for v in vals]
        delta = sum((p.astype(F32) * g).sum(axis=0, keepdims=True) for p, g in zip(low, gp))
        ds = [(p * (g - delta) * scale).astype(BF) for p, g in zip(probs, gp)]
        dq[i] = sum(
            lax.dot_general(d, k, tn, preferred_element_type=F32) for d, k in zip(ds, keys)
        )
        for terms, rows, acc, glob, behind, ahead, local in (
            (ds, qi, ak, sk, rkb, rka, lk),
            (low, ui, av, sv, rvb, rva, lv),
        ):
            w, g, r = [
                jnp.dot(t, rows, preferred_element_type=F32).reshape(-1, T, T) for t in terms
            ]
            acc[pl.ds(i, 3)] += w
            glob[...] += g
            r = r.astype(BF)
            for c in range(RANDOMS):
                k = RANDOMS * i + c
                send(plan[ME + k], k, r[c], behind, ahead, local)

    def send(src, k, v, behind, ahead, local):
        @pl.when(src < ROWBLK)
        def _():
            local[k] = v

        @pl.when((src >= ROWBLK) & (src < ROWBLK + FIN))
        def _():
            behind[src - ROWBLK] = v

        @pl.when(src >= ROWBLK + FIN)
        def _():
            ahead[src - ROWBLK - FIN] = v

    loop(NB, block)
    for glob, behind, ahead, local in ((sk, rkb, rka, lk), (sv, rvb, rva, lv)):
        for c in range(GLOBALS):
            k = RAND + c
            send(plan[ME + k], k, glob[c].astype(BF), behind, ahead, local)
    for which, (acc, out) in enumerate(((ak, gk), (av, gv))):
        out[...] = acc[pl.ds(1, NB)]
        eb[which] = acc[0].astype(BF)
        ea[which] = acc[NB + 1].astype(BF)


def return_kernel(plan, got_up, got_down, to_down, to_up):
    for base, got, out in ((FU, got_up, to_down), (FD, got_down, to_up)):

        def one(j):
            src = plan[base + j]

            @pl.when(src >= ROWBLK)
            def _():
                out[src - ROWBLK] = got[j]

        loop(FIN, one)


def total_kernel(plan, local, got_up, got_down, far_up, far_down, *refs):
    outs, acc = refs[:NZ], refs[NZ]
    acc[...] = jnp.zeros_like(acc)
    for base, n, got in (
        (ME, REQ, local),
        (FU, FIN, got_up),
        (FD, FIN, got_down),
        (RU, REL, far_up),
        (RD, REL, far_down),
    ):

        def one(j):
            src = plan[base + j]

            @pl.when((src >= 0) & (src < ROWBLK))
            def _():
                acc[src] += got[j].astype(F32)

        loop(n, one)
    for r, out in enumerate(outs):
        out[...] = acc[pl.ds(r * NB, NB)].astype(BF)


def per_device(queries, keys, values, grad_out, out_weight, random_blocks, global_blocks):
    position = lax.axis_index("seq")
    here = [(i, i // NZ, i % NZ) for i in range(NY * NZ)]

    def along_z(x, step):
        return lax.ppermute(x, "seq", [(i, y * NZ + (z + step) % NZ) for i, y, z in here])

    def along_y(x, step):
        return lax.ppermute(x, "seq", [(i, (y + step) % NY * NZ + z) for i, y, z in here])

    def along_seq(x, step):
        pairs = [(i, i + step) for i, _, _ in here if 0 <= i + step < NY * NZ]
        return lax.ppermute(x, "seq", pairs)

    q = queries.reshape(NB, T, T)
    own = [keys.reshape(NB, T, T), values.reshape(NB, T, T)]
    below = along_seq(jnp.stack([x[NB - 1] for x in own]), 1)
    above = along_seq(jnp.stack([x[0] for x in own]), -1)

    column = lax.dynamic_index_in_dim(
        random_blocks.reshape(NY, NZ, RAND), position % NZ, 1, keepdims=False
    )
    table = jnp.concatenate(
        [column, jnp.broadcast_to(global_blocks[None], (NY, GLOBALS))], axis=1
    ).reshape(-1)
    table = jnp.concatenate([table, jnp.stack([position // NZ, position % NZ])])
    plan = call(
        plan_kernel, jax.ShapeDtypeStruct((PLAN,), jnp.int32), [SMEM], smem_out=True, moved=2000
    )(table)

    upstream = lax.dot_general(
        lax.all_gather(grad_out, "head", axis=1, tiled=True),
        out_weight,
        (((1,), (1,)), ((), ())),
        preferred_element_type=F32,
    ).astype(BF).reshape(NB, T, T)

    rows, arrived = [], []
    for x, plus, minus in zip(own, (4, 3), (3, 4)):
        row = [x] + [None] * (NZ - 1)
        moving = x
        for s in range(1, plus + 1):
            moving = along_z(moving, 1)
            row[NZ - s] = moving
        moving = x
        for s in range(1, minus + 1):
            moving = along_z(moving, -1)
            row[s] = moving
        ru, rd, fu, fd = call(
            pack_kernel,
            (blocks(REL), blocks(REL), blocks(FIN), blocks(FIN)),
            [SMEM] + [VMEM] * NZ,
            moved=4 << 20,
        )(plan, *row)
        fu, fd = call(
            relay_kernel, (blocks(FIN), blocks(FIN)), [SMEM] + [VMEM] * 4, moved=3 << 20
        )(plan, along_y(ru, 1), along_y(rd, -1), fu, fd)
        arrived += [along_y(fu, 1), along_y(fd, -1)]
        rows += row

    dq, gk, gv, eb, ea, rkb, rka, rvb, rva, lk, lv = call(
        attention_kernel,
        (blocks(NB, F32), blocks(NB, F32), blocks(NB, F32), blocks(2), blocks(2))
        + (blocks(FIN),) * 4
        + (blocks(REQ),) * 2,
        [SMEM] + [VMEM] * (2 * NZ + 8),
        scratch=[pltpu.VMEM((NB + 2 + REQ, T, T), BF)] * 2
        + [pltpu.VMEM((NB + 2, T, T), F32)] * 2
        + [pltpu.VMEM((GLOBALS, T, T), F32)] * 2,
        flops=2 * 6 * 64 * T**3,
        moved=12 << 20,
    )(plan, q, upstream, *rows, below, above, *arrived)

    from_below = along_seq(ea, 1)
    from_above = along_seq(eb, -1)
    outs = []
    for which, (grad, behind, ahead, local, plus, minus) in enumerate(
        ((gk, rkb, rka, lk, 4, 3), (gv, rvb, rva, lv, 3, 4))
    ):
        got_up, got_down = along_y(behind, -1), along_y(ahead, 1)
        to_down, to_up = call(
            return_kernel, (blocks(REL), blocks(REL)), [SMEM, VMEM, VMEM], moved=2 << 20
        )(plan, got_up, got_down)
        far_up, far_down = along_y(to_down, -1), along_y(to_up, 1)
        parts = call(
            total_kernel,
            (blocks(NB),) * NZ,
            [SMEM] + [VMEM] * 5,
            scratch=[pltpu.VMEM((ROWBLK, T, T), F32)],
            moved=5 << 20,
        )(plan, local, got_up, got_down, far_up, far_down)
        sums = []
        for step, count in ((1, plus), (-1, minus)):
            moving = along_z(parts[step * count % NZ], step)
            for s in range(count - 1, 0, -1):
                moving = moving.astype(F32) + parts[step * s % NZ].astype(F32)
                moving = along_z(moving.astype(BF), step)
            sums.append(moving)
        out = grad + parts[0].astype(F32) + sums[0].astype(F32) + sums[1].astype(F32)
        out = out.at[0].add(from_below[which].astype(F32))
        out = out.at[NB - 1].add(from_above[which].astype(F32))
        outs.append(out.reshape(NB * T, T))
    return dq.reshape(NB * T, T), outs[0], outs[1]


def solution(mesh):
    return jax.shard_map(
        per_device,
        mesh=mesh,
        in_specs=(P("seq", "head"),) * 4 + (P("head", None), P(), P()),
        out_specs=(P("seq", "head"),) * 3,
        check_vma=False,
    )
```

```python
import math

import jax
import jax.numpy as jnp
from jax import lax
from jax.experimental import pallas as pl
from jax.experimental.pallas import tpu as pltpu
from jax.sharding import PartitionSpec as P

T = 128
GLOBALS = 2
RANDOMS = 3
NB = 8
NY = 4
NZ = 8
RAND = NB * RANDOMS
REQ = RAND + GLOBALS + 2
BEFORE, AFTER = REQ - 2, REQ - 1
ROWBLK = NZ * NB
FIN = 19
REL = 9

RU, RD = 0, REL
FU, FD = 2 * REL, 2 * REL + FIN
ME = 2 * REL + 2 * FIN
PLAN = ME + REQ + 2

BF = jnp.bfloat16
F32 = jnp.float32
VMEM = pl.BlockSpec(memory_space=pltpu.VMEM)
SMEM = pl.BlockSpec(memory_space=pltpu.SMEM)


def call(kernel, outs, ins, scratch=(), smem_out=False, outs_at=None, flops=0, moved=0, limit=48):
    return pl.pallas_call(
        kernel,
        out_shape=outs,
        in_specs=ins,
        out_specs=outs_at or jax.tree.map(lambda _: SMEM if smem_out else VMEM, outs),
        scratch_shapes=list(scratch),
        cost_estimate=pl.CostEstimate(flops=flops, bytes_accessed=moved, transcendentals=0),
        compiler_params=pltpu.CompilerParams(vmem_limit_bytes=limit * 1024 * 1024),
    )


def blocks(n, dtype=BF):
    return jax.ShapeDtypeStruct((n, T, T), dtype)


def plan_kernel(tab, plan):
    y, z = tab[NY * REQ], tab[NY * REQ + 1]

    def clear(j, c):
        plan[j] = -1
        return c

    lax.fori_loop(0, ME, clear, 0)
    plan[ME + REQ] = y
    plan[ME + REQ + 1] = z
    for off in range(NY):
        yd = (y + off) & (NY - 1)

        def where(k):
            b = tab[yd * REQ + k]
            far = ((b >> 6) - yd) & (NY - 1)
            return far, ((((b >> 3) - z) & (NZ - 1)) << 3) | (b & 7)

        def count(k, c):
            far, _ = where(k)
            return tuple(n + (far == r).astype(jnp.int32) for n, r in zip(c, (1, 2, 3)))

        zero = jnp.int32(0)
        ahead, across, behind = lax.fori_loop(0, REQ, count, (zero, zero, zero))
        low = jnp.maximum(jnp.maximum(across - REL, ahead + across - FIN), 0)
        high = jnp.minimum(jnp.minimum(across, REL), FIN - behind)
        via = jnp.minimum(jnp.maximum(across >> 1, low), high)

        def place(k, c):
            used_ahead, used_across, used_behind = c
            far, src = where(k)
            is1, is2, is3 = far == 1, far == 2, far == 3
            first = used_across < via
            down_slot = jnp.where(is3, used_behind, behind + used_across)
            up_slot = jnp.where(is1, used_ahead, ahead + used_across - via)
            from_behind = is3 | (is2 & first)
            from_ahead = is1 | (is2 & jnp.logical_not(first))
            if off == 0:
                plan[ME + k] = jnp.where(
                    from_behind,
                    ROWBLK + down_slot,
                    jnp.where(from_ahead, ROWBLK + FIN + up_slot, src),
                )
            elif off == 1:

                @pl.when(from_behind)
                def _():
                    plan[FU + down_slot] = jnp.where(is3, src, ROWBLK + used_across)
            elif off == 3:

                @pl.when(from_ahead)
                def _():
                    plan[FD + up_slot] = jnp.where(is1, src, ROWBLK + used_across - via)
            else:

                @pl.when(is2)
                def _():
                    plan[jnp.where(first, RU + used_across, RD + used_across - via)] = src

            return (
                used_ahead + is1.astype(jnp.int32),
                used_across + is2.astype(jnp.int32),
                used_behind + is3.astype(jnp.int32),
            )

        lax.fori_loop(0, REQ, place, (zero, zero, zero))


def loop(n, body):
    def step(j, c):
        body(j)
        return c

    lax.fori_loop(0, n, step, 0)


def gather_row(full, pieces):
    for r, piece in enumerate(pieces):
        full[pl.ds(r * NB, NB)] = piece[...]


def pack_kernel(plan, *refs):
    pieces, (ru, rd, fu, fd, full) = refs[:NZ], refs[NZ:]
    gather_row(full, pieces)
    for base, n, out in ((RU, REL, ru), (RD, REL, rd), (FU, FIN, fu), (FD, FIN, fd)):

        def one(j):
            src = plan[base + j]
            out[j] = full[jnp.where((src < 0) | (src >= ROWBLK), 0, src)]

        loop(n, one)


def relay_kernel(plan, got_up, got_down, fu_in, fd_in, fu, fd):
    for base, got, into, out in ((FU, got_up, fu_in, fu), (FD, got_down, fd_in, fd)):
        out[...] = into[...]

        def one(j):
            src = plan[base + j]

            @pl.when(src >= ROWBLK)
            def _():
                out[j] = got[src - ROWBLK]

        loop(FIN, one)


NT = (((1,), (1,)), ((), ()))
TN = (((0,), (0,)), ((), ()))
SCALE = 1.0 / math.sqrt(T)


def collect(plan, full, pieces, behind, ahead, every):
    gather_row(full, pieces)
    full[pl.ds(ROWBLK, FIN)] = behind[...]
    full[pl.ds(ROWBLK + FIN, FIN)] = ahead[...]
    every[0] = full[plan[ME + BEFORE]]
    every[pl.ds(1, NB)] = pieces[0][...]
    every[NB + 1] = full[plan[ME + AFTER]]

    def one(k):
        every[NB + 2 + k] = full[plan[ME + k]]

    loop(RAND + GLOBALS, one)


def slots(every, i):
    spans = (
        (i, 3),
        (NB + 2 + RAND, GLOBALS),
        (NB + 2 + RANDOMS * i, RANDOMS),
    )
    return [every[pl.ds(s, n)].reshape(n * T, T) for s, n in spans]


def put_term(plan, back, k, v):
    at = plan[ME + k]
    back[jnp.where(at < ROWBLK, 2 * FIN + k, at - ROWBLK)] = v


def add_terms(plan, i, terms, rows, acc, glob, back):
    w, g, r = [jnp.dot(t, rows, preferred_element_type=F32).reshape(-1, T, T) for t in terms]
    acc[pl.ds(i, 3)] += w
    glob[...] += g
    r = r.astype(BF)
    for c in range(RANDOMS):
        put_term(plan, back, RANDOMS * i + c, r[c])


def finish(plan, acc, glob, back, grad, behind, ahead, local):
    for c in range(GLOBALS):
        put_term(plan, back, RAND + c, glob[c].astype(BF))
    put_term(plan, back, BEFORE, acc[0].astype(BF))
    put_term(plan, back, AFTER, acc[NB + 1].astype(BF))
    grad[...] = acc[pl.ds(1, NB)]
    behind[...] = back[pl.ds(0, FIN)]
    ahead[...] = back[pl.ds(FIN, FIN)]
    local[...] = back[pl.ds(2 * FIN, REQ)]


def probs_kernel(plan, q, u, *refs):
    pieces, (behind, ahead) = refs[:NZ], refs[NZ : NZ + 2]
    probs_out, every, grad, tb, ta, tl, full, acc, glob, back, held, sems = refs[NZ + 2 :]
    at = plan[ME + REQ] * NZ + plan[ME + REQ + 1]
    collect(plan, full, pieces, behind, ahead, every)
    acc[...] = jnp.zeros_like(acc)
    glob[...] = jnp.zeros_like(glob)

    def save(i):
        return pltpu.make_async_copy(held.at[i], probs_out.at[i], sems.at[i])

    def block(i):
        qi, ui = q[i], u[i]
        no_before = jnp.where((at == 0) & (i == 0), -1e30, 0.0)
        no_after = jnp.where((at == NY * NZ - 1) & (i == NB - 1), -1e30, 0.0)
        logits = [
            lax.dot_general(k, qi, NT, preferred_element_type=F32) * (SCALE * math.log2(math.e))
            for k in slots(every, i)
        ]
        window = logits[0]
        logits[0] = jnp.concatenate(
            [window[:T] + no_before, window[T : 2 * T], window[2 * T :] + no_after], axis=0
        )
        top = logits[0].max(axis=0, keepdims=True)
        for x in logits[1:]:
            top = jnp.maximum(top, x.max(axis=0, keepdims=True))
        weights = [jnp.exp2(x - top) for x in logits]
        total = sum(w.sum(axis=0, keepdims=True) for w in weights)
        inverse = 1.0 / total
        probs = [w * inverse for w in weights]
        row = 0
        for p in probs:
            held[i, pl.ds(row, p.shape[0])] = p
            row += p.shape[0]
        save(i).start()
        add_terms(plan, i, [p.astype(BF) for p in probs], ui, acc, glob, back)

    loop(NB, block)
    finish(plan, acc, glob, back, grad, tb, ta, tl)
    loop(NB, lambda i: save(i).wait())


def scores_kernel(plan, q, u, every, probs_in, *refs):
    pieces, (behind, ahead) = refs[:NZ], refs[NZ : NZ + 2]
    dq, grad, tb, ta, tl, full, values, acc, glob, back, held, sems = refs[NZ + 2 :]

    def fetch(i):
        return pltpu.make_async_copy(probs_in.at[i], held.at[i], sems.at[i])

    loop(NB, lambda i: fetch(i).start())
    collect(plan, full, pieces, behind, ahead, values)
    acc[...] = jnp.zeros_like(acc)
    glob[...] = jnp.zeros_like(glob)

    def block(i):
        qi, ui = q[i], u[i]
        gp = [
            lax.dot_general(v, ui, NT, preferred_element_type=F32) for v in slots(values, i)
        ]
        fetch(i).wait()
        probs, row = [], 0
        for g in gp:
            probs.append(held[i, pl.ds(row, g.shape[0])])
            row += g.shape[0]
        delta = sum(
            (p.astype(BF).astype(F32) * g).sum(axis=0, keepdims=True) for p, g in zip(probs, gp)
        )
        ds = [(p * (g - delta) * SCALE).astype(BF) for p, g in zip(probs, gp)]
        dq[i] = sum(
            lax.dot_general(d, k, TN, preferred_element_type=F32)
            for d, k in zip(ds, slots(every, i))
        )
        add_terms(plan, i, ds, qi, acc, glob, back)

    loop(NB, block)
    finish(plan, acc, glob, back, grad, tb, ta, tl)


def return_kernel(plan, got_up, got_down, to_down, to_up):
    for base, got, out in ((FU, got_up, to_down), (FD, got_down, to_up)):

        def one(j):
            src = plan[base + j]

            @pl.when(src >= ROWBLK)
            def _():
                out[src - ROWBLK] = got[j]

        loop(FIN, one)


def total_kernel(plan, local, got_up, got_down, far_up, far_down, *refs):
    outs, acc = refs[:NZ], refs[NZ]
    acc[...] = jnp.zeros_like(acc)
    for base, n, got in (
        (ME, REQ, local),
        (FU, FIN, got_up),
        (FD, FIN, got_down),
        (RU, REL, far_up),
        (RD, REL, far_down),
    ):

        def one(j):
            src = plan[base + j]

            @pl.when((src >= 0) & (src < ROWBLK))
            def _():
                acc[src] += got[j].astype(F32)

        loop(n, one)
    for r, out in enumerate(outs):
        out[...] = acc[pl.ds(r * NB, NB)].astype(BF)


def after(x, *earlier):
    return lax.optimization_barrier((x,) + earlier)[0]


def per_device(queries, keys, values, grad_out, out_weight, random_blocks, global_blocks):
    position = lax.axis_index("seq")
    here = [(i, i // NZ, i % NZ) for i in range(NY * NZ)]

    def along_z(x, step):
        return lax.ppermute(x, "seq", [(i, y * NZ + (z + step) % NZ) for i, y, z in here])

    def along_y(x, step):
        return lax.ppermute(x, "seq", [(i, (y + step) % NY * NZ + z) for i, y, z in here])

    q = queries.reshape(NB, T, T)

    column = lax.dynamic_index_in_dim(
        random_blocks.reshape(NY, NZ, RAND), position % NZ, 1, keepdims=False
    )
    first = (jnp.arange(NY) * NZ + position % NZ)[:, None] * NB
    edges = jnp.concatenate(
        [jnp.maximum(first - 1, 0), jnp.minimum(first + NB, NY * NZ * NB - 1)], axis=1
    )
    table = jnp.concatenate(
        [column, jnp.broadcast_to(global_blocks[None], (NY, GLOBALS)), edges], axis=1
    ).reshape(-1)
    table = jnp.concatenate([table, jnp.stack([position // NZ, position % NZ])])
    plan = call(
        plan_kernel, jax.ShapeDtypeStruct((PLAN,), jnp.int32), [SMEM], smem_out=True, moved=2000
    )(table)

    upstream = lax.dot_general(
        lax.all_gather(grad_out, "head", axis=1, tiled=True),
        out_weight,
        (((1,), (1,)), ((), ())),
        preferred_element_type=F32,
    ).astype(BF).reshape(NB, T, T)

    def pack(row):
        return call(
            pack_kernel,
            (blocks(REL), blocks(REL), blocks(FIN), blocks(FIN)),
            [SMEM] + [VMEM] * NZ,
            scratch=[pltpu.VMEM((ROWBLK, T, T), BF)],
            moved=4 << 20,
        )(plan, *row)

    def spread(ru, rd, fu, fd):
        far = along_y(ru, 1), along_y(rd, -1)
        fu, fd = call(
            relay_kernel, (blocks(FIN), blocks(FIN)), [SMEM] + [VMEM] * 4, moved=3 << 20
        )(plan, *far, fu, fd)
        return (along_y(fu, 1), along_y(fd, -1)), far

    def hop_back(behind, ahead, *earlier):
        return along_y(after(behind, *earlier), -1), along_y(after(ahead, *earlier), 1)

    def relay_back(got_up, got_down, *earlier):
        return call(
            return_kernel, (blocks(REL), blocks(REL)), [SMEM, VMEM, VMEM], moved=2 << 20
        )(plan, after(got_up, *earlier), got_down)

    def add_up(local, got_up, got_down, to_down, to_up):
        return call(
            total_kernel,
            (blocks(NB),) * NZ,
            [SMEM] + [VMEM] * 5,
            scratch=[pltpu.VMEM((ROWBLK, T, T), F32)],
            moved=5 << 20,
        )(plan, local, got_up, got_down, along_y(to_down, -1), along_y(to_up, 1))

    def ring_sum(grad, parts, plus, minus):
        sums = []
        for step, count in ((1, plus), (-1, minus)):
            moving = along_z(parts[step * count % NZ], step)
            for s in range(count - 1, 0, -1):
                moving = moving.astype(F32) + parts[step * s % NZ].astype(F32)
                moving = along_z(moving.astype(BF), step)
            sums.append(moving)
        out = grad + parts[0].astype(F32) + sums[0].astype(F32) + sums[1].astype(F32)
        return out.reshape(NB * T, T)

    scratch = [
        pltpu.VMEM((NB + 2, T, T), F32),
        pltpu.VMEM((GLOBALS, T, T), F32),
        pltpu.VMEM((2 * FIN + REQ, T, T), BF),
        pltpu.VMEM((NB, 8 * T, T), F32),
        pltpu.SemaphoreType.DMA((NB,)),
    ]
    full = pltpu.VMEM((ROWBLK + 2 * FIN, T, T), BF)
    every = NB + 2 + RAND + GLOBALS
    grads = (blocks(NB, F32), blocks(FIN), blocks(FIN), blocks(REQ))
    anywhere = pl.BlockSpec(memory_space=pl.ANY)

    krow = [keys.reshape(NB, T, T)] + [None] * (NZ - 1)
    vrow = [values.reshape(NB, T, T)] + [None] * (NZ - 1)

    def step(row, s, *earlier, plus=True, minus=True):
        up, down = row[(NZ + 1 - s) % NZ], row[s - 1]
        if plus:
            row[NZ - s] = along_z(after(up, *earlier) if earlier else up, 1)
        if minus:
            row[s] = along_z(after(down, *earlier) if earlier else down, -1)

    step(krow, 1)
    step(vrow, 1)
    step(krow, 2)
    step(vrow, 2)
    step(krow, 3, plan)
    step(vrow, 3)
    step(krow, 4, minus=False)
    step(vrow, 4, plus=False)
    kpack = pack(krow)
    vpack = pack(vrow)
    kfin, _ = spread(*kpack)
    vfin, _ = spread(*vpack)

    probs, kall, gv, *vback = call(
        probs_kernel,
        (jax.ShapeDtypeStruct((NB, 8 * T, T), F32), blocks(every)) + grads,
        [SMEM] + [VMEM] * (2 + NZ + 2),
        outs_at=[anywhere] + [VMEM] * 5,
        scratch=[full] + scratch,
        flops=2 * 2 * 64 * T**3,
        moved=12 << 20,
    )(plan, q, upstream, *krow, *kfin)
    dq, gk, *kback = call(
        scores_kernel,
        (blocks(NB, F32),) + grads,
        [SMEM] + [VMEM] * 3 + [anywhere] + [VMEM] * (NZ + 2),
        scratch=[full, pltpu.VMEM((every, T, T), BF)] + scratch,
        flops=2 * 3 * 64 * T**3,
        moved=12 << 20,
    )(plan, q, upstream, kall, probs, *vrow, *vfin)

    vgot = hop_back(*vback[:2])
    vfar = relay_back(*vgot)
    kgot = hop_back(*kback[:2], vfar[0])
    vparts = add_up(vback[2], *vgot, *vfar)
    kfar = relay_back(*kgot, vparts[0])
    kparts = add_up(kback[2], *kgot, *kfar)
    dv = ring_sum(gv, vparts, 3, 4)
    dk = ring_sum(gk, kparts, 4, 3)
    return dq.reshape(NB * T, T), dk, dv


def solution(mesh):
    return jax.shard_map(
        per_device,
        mesh=mesh,
        in_specs=(P("seq", "head"),) * 4 + (P("head", None), P(), P()),
        out_specs=(P("seq", "head"),) * 3,
        check_vma=False,
    )
```

```python
import math

import jax
import jax.numpy as jnp
from jax import lax
from jax.experimental import pallas as pl
from jax.experimental.pallas import tpu as pltpu
from jax.sharding import PartitionSpec as P

T = 128
GLOBALS = 2
RANDOMS = 3
NB = 8
NY = 4
NZ = 8
RAND = NB * RANDOMS
REQ = RAND + GLOBALS + 2
BEFORE, AFTER = REQ - 2, REQ - 1
ROWBLK = NZ * NB
FIN = 19
REL = 9

RU, RD = 0, REL
FU, FD = 2 * REL, 2 * REL + FIN
ME = 2 * REL + 2 * FIN
PLAN = ME + REQ + 2

BF = jnp.bfloat16
F32 = jnp.float32
VMEM = pl.BlockSpec(memory_space=pltpu.VMEM)
SMEM = pl.BlockSpec(memory_space=pltpu.SMEM)


def call(kernel, outs, ins, scratch=(), smem_out=False, outs_at=None, flops=0, moved=0, limit=48):
    return pl.pallas_call(
        kernel,
        out_shape=outs,
        in_specs=ins,
        out_specs=outs_at or jax.tree.map(lambda _: SMEM if smem_out else VMEM, outs),
        scratch_shapes=list(scratch),
        cost_estimate=pl.CostEstimate(flops=flops, bytes_accessed=moved, transcendentals=0),
        compiler_params=pltpu.CompilerParams(vmem_limit_bytes=limit * 1024 * 1024),
    )


def blocks(n, dtype=BF):
    return jax.ShapeDtypeStruct((n, T, T), dtype)


def plan_kernel(tab, plan):
    y, z = tab[NY * REQ], tab[NY * REQ + 1]

    def clear(j, c):
        plan[j] = -1
        return c

    lax.fori_loop(0, ME, clear, 0)
    plan[ME + REQ] = y
    plan[ME + REQ + 1] = z
    for off in range(NY):
        yd = (y + off) & (NY - 1)

        def where(k):
            b = tab[yd * REQ + k]
            far = ((b >> 6) - yd) & (NY - 1)
            return far, ((((b >> 3) - z) & (NZ - 1)) << 3) | (b & 7)

        def count(k, c):
            far, _ = where(k)
            return tuple(n + (far == r).astype(jnp.int32) for n, r in zip(c, (1, 2, 3)))

        zero = jnp.int32(0)
        ahead, across, behind = lax.fori_loop(0, REQ, count, (zero, zero, zero))
        low = jnp.maximum(jnp.maximum(across - REL, ahead + across - FIN), 0)
        high = jnp.minimum(jnp.minimum(across, REL), FIN - behind)
        via = jnp.minimum(jnp.maximum(across >> 1, low), high)

        def place(k, c):
            used_ahead, used_across, used_behind = c
            far, src = where(k)
            is1, is2, is3 = far == 1, far == 2, far == 3
            first = used_across < via
            down_slot = jnp.where(is3, used_behind, behind + used_across)
            up_slot = jnp.where(is1, used_ahead, ahead + used_across - via)
            from_behind = is3 | (is2 & first)
            from_ahead = is1 | (is2 & jnp.logical_not(first))
            if off == 0:
                plan[ME + k] = jnp.where(
                    from_behind,
                    ROWBLK + down_slot,
                    jnp.where(from_ahead, ROWBLK + FIN + up_slot, src),
                )
            elif off == 1:

                @pl.when(from_behind)
                def _():
                    plan[FU + down_slot] = jnp.where(is3, src, ROWBLK + used_across)
            elif off == 3:

                @pl.when(from_ahead)
                def _():
                    plan[FD + up_slot] = jnp.where(is1, src, ROWBLK + used_across - via)
            else:

                @pl.when(is2)
                def _():
                    plan[jnp.where(first, RU + used_across, RD + used_across - via)] = src

            return (
                used_ahead + is1.astype(jnp.int32),
                used_across + is2.astype(jnp.int32),
                used_behind + is3.astype(jnp.int32),
            )

        lax.fori_loop(0, REQ, place, (zero, zero, zero))


def loop(n, body):
    def step(j, c):
        body(j)
        return c

    lax.fori_loop(0, n, step, 0)


def gather_row(full, pieces):
    for r, piece in enumerate(pieces):
        full[pl.ds(r * NB, NB)] = piece[...]


def pack_kernel(plan, *refs):
    pieces, (ru, rd, fu, fd, full) = refs[:NZ], refs[NZ:]
    gather_row(full, pieces)
    for base, n, out in ((RU, REL, ru), (RD, REL, rd), (FU, FIN, fu), (FD, FIN, fd)):

        def one(j):
            src = plan[base + j]
            out[j] = full[jnp.where((src < 0) | (src >= ROWBLK), 0, src)]

        loop(n, one)


def relay_kernel(plan, got_up, got_down, fu_in, fd_in, fu, fd):
    for base, got, into, out in ((FU, got_up, fu_in, fu), (FD, got_down, fd_in, fd)):
        out[...] = into[...]

        def one(j):
            src = plan[base + j]

            @pl.when(src >= ROWBLK)
            def _():
                out[j] = got[src - ROWBLK]

        loop(FIN, one)


NT = (((1,), (1,)), ((), ()))
TN = (((0,), (0,)), ((), ()))
SCALE = 1.0 / math.sqrt(T)


def collect(plan, full, pieces, behind, ahead, every):
    gather_row(full, pieces)
    full[pl.ds(ROWBLK, FIN)] = behind[...]
    full[pl.ds(ROWBLK + FIN, FIN)] = ahead[...]
    every[0] = full[plan[ME + BEFORE]]
    every[pl.ds(1, NB)] = pieces[0][...]
    every[NB + 1] = full[plan[ME + AFTER]]

    def one(k):
        every[NB + 2 + k] = full[plan[ME + k]]

    loop(RAND + GLOBALS, one)


def slots(every, i):
    spans = (
        (i, 3),
        (NB + 2 + RAND, GLOBALS),
        (NB + 2 + RANDOMS * i, RANDOMS),
    )
    return [every[pl.ds(s, n)].reshape(n * T, T) for s, n in spans]


def put_term(plan, back, k, v):
    at = plan[ME + k]
    back[jnp.where(at < ROWBLK, 2 * FIN + k, at - ROWBLK)] = v


def add_terms(plan, i, terms, rows, acc, glob, back):
    w, g, r = [jnp.dot(t, rows, preferred_element_type=F32).reshape(-1, T, T) for t in terms]
    acc[pl.ds(i, 3)] += w
    glob[...] += g
    r = r.astype(BF)
    for c in range(RANDOMS):
        put_term(plan, back, RANDOMS * i + c, r[c])


def finish(plan, acc, glob, back, grad, behind, ahead, local):
    for c in range(GLOBALS):
        put_term(plan, back, RAND + c, glob[c].astype(BF))
    put_term(plan, back, BEFORE, acc[0].astype(BF))
    put_term(plan, back, AFTER, acc[NB + 1].astype(BF))
    grad[...] = acc[pl.ds(1, NB)]
    behind[...] = back[pl.ds(0, FIN)]
    ahead[...] = back[pl.ds(FIN, FIN)]
    local[...] = back[pl.ds(2 * FIN, REQ)]


def probs_kernel(plan, q, u, *refs):
    pieces, (behind, ahead) = refs[:NZ], refs[NZ : NZ + 2]
    probs_out, every, grad, tb, ta, tl, full, acc, glob, back, held, sems = refs[NZ + 2 :]
    at = plan[ME + REQ] * NZ + plan[ME + REQ + 1]
    collect(plan, full, pieces, behind, ahead, every)
    acc[...] = jnp.zeros_like(acc)
    glob[...] = jnp.zeros_like(glob)

    def save(i):
        return pltpu.make_async_copy(held.at[i], probs_out.at[i], sems.at[i])

    def block(i):
        qi, ui = q[i], u[i]
        no_before = jnp.where((at == 0) & (i == 0), -1e30, 0.0)
        no_after = jnp.where((at == NY * NZ - 1) & (i == NB - 1), -1e30, 0.0)
        logits = [
            lax.dot_general(k, qi, NT, preferred_element_type=F32) * (SCALE * math.log2(math.e))
            for k in slots(every, i)
        ]
        window = logits[0]
        logits[0] = jnp.concatenate(
            [window[:T] + no_before, window[T : 2 * T], window[2 * T :] + no_after], axis=0
        )
        top = logits[0].max(axis=0, keepdims=True)
        for x in logits[1:]:
            top = jnp.maximum(top, x.max(axis=0, keepdims=True))
        weights = [jnp.exp2(x - top) for x in logits]
        total = sum(w.sum(axis=0, keepdims=True) for w in weights)
        inverse = 1.0 / total
        probs = [w * inverse for w in weights]
        row = 0
        for p in probs:
            held[i, pl.ds(row, p.shape[0])] = p
            row += p.shape[0]
        save(i).start()
        add_terms(plan, i, [p.astype(BF) for p in probs], ui, acc, glob, back)

    loop(NB, block)
    finish(plan, acc, glob, back, grad, tb, ta, tl)
    loop(NB, lambda i: save(i).wait())


def scores_kernel(plan, q, u, every, probs_in, *refs):
    pieces, (behind, ahead) = refs[:NZ], refs[NZ : NZ + 2]
    dq, grad, tb, ta, tl, full, values, acc, glob, back, held, sems = refs[NZ + 2 :]

    def fetch(i):
        return pltpu.make_async_copy(probs_in.at[i], held.at[i], sems.at[i])

    loop(NB, lambda i: fetch(i).start())
    collect(plan, full, pieces, behind, ahead, values)
    acc[...] = jnp.zeros_like(acc)
    glob[...] = jnp.zeros_like(glob)

    def block(i):
        qi, ui = q[i], u[i]
        gp = [
            lax.dot_general(v, ui, NT, preferred_element_type=F32) for v in slots(values, i)
        ]
        fetch(i).wait()
        probs, row = [], 0
        for g in gp:
            probs.append(held[i, pl.ds(row, g.shape[0])])
            row += g.shape[0]
        delta = sum(
            (p.astype(BF).astype(F32) * g).sum(axis=0, keepdims=True) for p, g in zip(probs, gp)
        )
        ds = [(p * (g - delta) * SCALE).astype(BF) for p, g in zip(probs, gp)]
        dq[i] = sum(
            lax.dot_general(d, k, TN, preferred_element_type=F32)
            for d, k in zip(ds, slots(every, i))
        )
        add_terms(plan, i, ds, qi, acc, glob, back)

    loop(NB, block)
    finish(plan, acc, glob, back, grad, tb, ta, tl)


def return_kernel(plan, got_up, got_down, to_down, to_up):
    for base, got, out in ((FU, got_up, to_down), (FD, got_down, to_up)):

        def one(j):
            src = plan[base + j]

            @pl.when(src >= ROWBLK)
            def _():
                out[src - ROWBLK] = got[j]

        loop(FIN, one)


def total_kernel(plan, local, got_up, got_down, far_up, far_down, *refs):
    outs, acc = refs[:NZ], refs[NZ]
    acc[...] = jnp.zeros_like(acc)
    for base, n, got in (
        (ME, REQ, local),
        (FU, FIN, got_up),
        (FD, FIN, got_down),
        (RU, REL, far_up),
        (RD, REL, far_down),
    ):

        def one(j):
            src = plan[base + j]

            @pl.when((src >= 0) & (src < ROWBLK))
            def _():
                acc[src] += got[j].astype(F32)

        loop(n, one)
    for r, out in enumerate(outs):
        out[...] = acc[pl.ds(r * NB, NB)].astype(BF)


def after(x, *earlier):
    return lax.optimization_barrier((x,) + earlier)[0]


def per_device(queries, keys, values, grad_out, out_weight, random_blocks, global_blocks):
    position = lax.axis_index("seq")
    here = [(i, i // NZ, i % NZ) for i in range(NY * NZ)]

    def along_z(x, step):
        return lax.ppermute(x, "seq", [(i, y * NZ + (z + step) % NZ) for i, y, z in here])

    def along_y(x, step):
        return lax.ppermute(x, "seq", [(i, (y + step) % NY * NZ + z) for i, y, z in here])

    q = queries.reshape(NB, T, T)

    column = lax.dynamic_index_in_dim(
        random_blocks.reshape(NY, NZ, RAND), position % NZ, 1, keepdims=False
    )
    first = (jnp.arange(NY) * NZ + position % NZ)[:, None] * NB
    edges = jnp.concatenate(
        [jnp.maximum(first - 1, 0), jnp.minimum(first + NB, NY * NZ * NB - 1)], axis=1
    )
    table = jnp.concatenate(
        [column, jnp.broadcast_to(global_blocks[None], (NY, GLOBALS)), edges], axis=1
    ).reshape(-1)
    table = jnp.concatenate([table, jnp.stack([position // NZ, position % NZ])])
    plan = call(
        plan_kernel, jax.ShapeDtypeStruct((PLAN,), jnp.int32), [SMEM], smem_out=True, moved=2000
    )(table)

    upstream = lax.dot_general(
        lax.all_gather(grad_out, "head", axis=1, tiled=True),
        out_weight,
        (((1,), (1,)), ((), ())),
        preferred_element_type=F32,
    ).astype(BF).reshape(NB, T, T)

    def pack(row):
        return call(
            pack_kernel,
            (blocks(REL), blocks(REL), blocks(FIN), blocks(FIN)),
            [SMEM] + [VMEM] * NZ,
            scratch=[pltpu.VMEM((ROWBLK, T, T), BF)],
            moved=4 << 20,
        )(plan, *row)

    def spread(ru, rd, fu, fd):
        far = along_y(ru, 1), along_y(rd, -1)
        fu, fd = call(
            relay_kernel, (blocks(FIN), blocks(FIN)), [SMEM] + [VMEM] * 4, moved=3 << 20
        )(plan, *far, fu, fd)
        return (along_y(fu, 1), along_y(fd, -1)), fu

    def hop_back(behind, ahead, *earlier):
        return along_y(after(behind, *earlier), -1), along_y(after(ahead, *earlier), 1)

    def relay_back(got_up, got_down, *earlier):
        to_down, to_up = call(
            return_kernel, (blocks(REL), blocks(REL)), [SMEM, VMEM, VMEM], moved=2 << 20
        )(plan, after(got_up, *earlier), got_down)
        return along_y(to_down, -1), along_y(to_up, 1)

    def add_up(local, got_up, got_down, far_up, far_down):
        return call(
            total_kernel,
            (blocks(NB),) * NZ,
            [SMEM] + [VMEM] * 5,
            scratch=[pltpu.VMEM((ROWBLK, T, T), F32)],
            moved=5 << 20,
        )(plan, local, got_up, got_down, far_up, far_down)

    def ring_start(parts, plus, minus):
        return [(parts, 1, plus, along_z(parts[plus], 1))] + [
            (parts, -1, minus, along_z(parts[NZ - minus], -1))
        ]

    def ring_add(rings):
        return [
            (moving.astype(F32) + parts[step * (left - 1) % NZ].astype(F32)).astype(BF)
            for parts, step, left, moving in rings
        ]

    def ring_next(rings, sums):
        return [
            (parts, step, left - 1, along_z(x, step))
            for (parts, step, left, _), x in zip(rings, sums)
        ]

    def ring_end(grad, rings):
        while any(left > 1 for _, _, left, _ in rings):
            more = [r for r in rings if r[2] > 1]
            rings = [r for r in rings if r[2] == 1] + ring_next(more, ring_add(more))
        out = grad + rings[0][0][0].astype(F32) + sum(r[3].astype(F32) for r in rings)
        return out.reshape(NB * T, T)

    scratch = [
        pltpu.VMEM((NB + 2, T, T), F32),
        pltpu.VMEM((GLOBALS, T, T), F32),
        pltpu.VMEM((2 * FIN + REQ, T, T), BF),
        pltpu.VMEM((NB, 8 * T, T), F32),
        pltpu.SemaphoreType.DMA((NB,)),
    ]
    full = pltpu.VMEM((ROWBLK + 2 * FIN, T, T), BF)
    every = NB + 2 + RAND + GLOBALS
    grads = (blocks(NB, F32), blocks(FIN), blocks(FIN), blocks(REQ))
    anywhere = pl.BlockSpec(memory_space=pl.ANY)

    krow = [keys.reshape(NB, T, T)] + [None] * (NZ - 1)
    vrow = [values.reshape(NB, T, T)] + [None] * (NZ - 1)

    def step(row, s, *earlier, plus=True, minus=True):
        up, down = row[(NZ + 1 - s) % NZ], row[s - 1]
        if plus:
            row[NZ - s] = along_z(after(up, *earlier) if earlier else up, 1)
        if minus:
            row[s] = along_z(after(down, *earlier) if earlier else down, -1)

    step(krow, 1)
    step(vrow, 1)
    step(krow, 2)
    step(vrow, 2)
    step(krow, 3, plan)
    step(vrow, 3)
    step(krow, 4, minus=False)
    step(vrow, 4, plus=False)
    kpack = pack(krow)
    vpack = pack(vrow)
    kfin, _ = spread(*kpack)
    vfin, vready = spread(*vpack)

    probs, kall, gv, *vback = call(
        probs_kernel,
        (jax.ShapeDtypeStruct((NB, 8 * T, T), F32), blocks(every)) + grads,
        [SMEM] + [VMEM] * (2 + NZ + 2),
        outs_at=[anywhere] + [VMEM] * 5,
        scratch=[full] + scratch,
        flops=2 * 2 * 64 * T**3,
        moved=12 << 20,
        limit=48,
    )(plan, after(q, vready), upstream, *krow, *kfin)
    dq, gk, *kback = call(
        scores_kernel,
        (blocks(NB, F32),) + grads,
        [SMEM] + [VMEM] * 3 + [anywhere] + [VMEM] * (NZ + 2),
        scratch=[full, pltpu.VMEM((every, T, T), BF)] + scratch,
        flops=2 * 3 * 64 * T**3,
        moved=12 << 20,
        limit=48,
    )(plan, q, upstream, kall, probs, *vrow, *vfin)

    vgot = hop_back(*vback[:2])
    vfar = relay_back(*vgot, kback[0])
    kgot = hop_back(*kback[:2], *vfar)
    vring = ring_start(add_up(vback[2], *vgot, *vfar), 3, 4)
    vsums = ring_add(vring)
    vring = ring_next(vring, vsums)
    kfar = relay_back(*kgot, *vsums)
    vsums = ring_add(vring)
    vring = ring_next(vring, vsums)
    kring = ring_start(add_up(after(kback[2], *vsums), *kgot, *kfar), 4, 3)
    dv = ring_end(gv, vring)
    dk = ring_end(gk, kring)
    return dq.reshape(NB * T, T), dk, dv


def solution(mesh):
    return jax.shard_map(
        per_device,
        mesh=mesh,
        in_specs=(P("seq", "head"),) * 4 + (P("head", None), P(), P()),
        out_specs=(P("seq", "head"),) * 3,
        check_vma=False,
    )
```

```python
import math

import jax
import jax.numpy as jnp
from jax import lax
from jax.experimental import pallas as pl
from jax.experimental.pallas import tpu as pltpu
from jax.sharding import PartitionSpec as P

T = 128
GLOBALS = 2
RANDOMS = 3
NB = 8
NY = 4
NZ = 8
RAND = NB * RANDOMS
REQ = RAND + GLOBALS + 2
BEFORE, AFTER = REQ - 2, REQ - 1
ROWBLK = NZ * NB
FIN = 19
REL = 9

RU, RD = 0, REL
FU, FD = 2 * REL, 2 * REL + FIN
ME = 2 * REL + 2 * FIN
PLAN = ME + REQ + 2

BF = jnp.bfloat16
F32 = jnp.float32
VMEM = pl.BlockSpec(memory_space=pltpu.VMEM)
SMEM = pl.BlockSpec(memory_space=pltpu.SMEM)


def call(kernel, outs, ins, scratch=(), smem_out=False, outs_at=None, flops=0, moved=0, limit=48):
    return pl.pallas_call(
        kernel,
        out_shape=outs,
        in_specs=ins,
        out_specs=outs_at or jax.tree.map(lambda _: SMEM if smem_out else VMEM, outs),
        scratch_shapes=list(scratch),
        cost_estimate=pl.CostEstimate(flops=flops, bytes_accessed=moved, transcendentals=0),
        compiler_params=pltpu.CompilerParams(vmem_limit_bytes=limit * 1024 * 1024),
    )


def blocks(n, dtype=BF):
    return jax.ShapeDtypeStruct((n, T, T), dtype)


def plan_kernel(tab, plan):
    y, z = tab[NY * REQ], tab[NY * REQ + 1]

    def clear(j, c):
        plan[j] = -1
        return c

    lax.fori_loop(0, ME, clear, 0)
    plan[ME + REQ] = y
    plan[ME + REQ + 1] = z
    for off in range(NY):
        yd = (y + off) & (NY - 1)

        def where(k):
            b = tab[yd * REQ + k]
            far = ((b >> 6) - yd) & (NY - 1)
            return far, ((((b >> 3) - z) & (NZ - 1)) << 3) | (b & 7)

        def count(k, c):
            far, _ = where(k)
            return tuple(n + (far == r).astype(jnp.int32) for n, r in zip(c, (1, 2, 3)))

        zero = jnp.int32(0)
        ahead, across, behind = lax.fori_loop(0, REQ, count, (zero, zero, zero))
        low = jnp.maximum(jnp.maximum(across - REL, ahead + across - FIN), 0)
        high = jnp.minimum(jnp.minimum(across, REL), FIN - behind)
        via = jnp.minimum(jnp.maximum(across >> 1, low), high)

        def place(k, c):
            used_ahead, used_across, used_behind = c
            far, src = where(k)
            is1, is2, is3 = far == 1, far == 2, far == 3
            first = used_across < via
            down_slot = jnp.where(is3, used_behind, behind + used_across)
            up_slot = jnp.where(is1, used_ahead, ahead + used_across - via)
            from_behind = is3 | (is2 & first)
            from_ahead = is1 | (is2 & jnp.logical_not(first))
            if off == 0:
                plan[ME + k] = jnp.where(
                    from_behind,
                    ROWBLK + down_slot,
                    jnp.where(from_ahead, ROWBLK + FIN + up_slot, src),
                )
            elif off == 1:

                @pl.when(from_behind)
                def _():
                    plan[FU + down_slot] = jnp.where(is3, src, ROWBLK + used_across)
            elif off == 3:

                @pl.when(from_ahead)
                def _():
                    plan[FD + up_slot] = jnp.where(is1, src, ROWBLK + used_across - via)
            else:

                @pl.when(is2)
                def _():
                    plan[jnp.where(first, RU + used_across, RD + used_across - via)] = src

            return (
                used_ahead + is1.astype(jnp.int32),
                used_across + is2.astype(jnp.int32),
                used_behind + is3.astype(jnp.int32),
            )

        lax.fori_loop(0, REQ, place, (zero, zero, zero))


def loop(n, body):
    def step(j, c):
        body(j)
        return c

    lax.fori_loop(0, n, step, 0)


def gather_row(full, pieces):
    for r, piece in enumerate(pieces):
        full[pl.ds(r * NB, NB)] = piece[...]


def pack_kernel(plan, *refs):
    pieces, (ru, rd, fu, fd, full) = refs[:NZ], refs[NZ:]
    gather_row(full, pieces)
    for base, n, out in ((RU, REL, ru), (RD, REL, rd), (FU, FIN, fu), (FD, FIN, fd)):

        def one(j):
            src = plan[base + j]
            out[j] = full[jnp.where((src < 0) | (src >= ROWBLK), 0, src)]

        loop(n, one)


def relay_kernel(plan, got_up, got_down, fu_in, fd_in, fu, fd):
    for base, got, into, out in ((FU, got_up, fu_in, fu), (FD, got_down, fd_in, fd)):
        out[...] = into[...]

        def one(j):
            src = plan[base + j]

            @pl.when(src >= ROWBLK)
            def _():
                out[j] = got[src - ROWBLK]

        loop(FIN, one)


NT = (((1,), (1,)), ((), ()))
TN = (((0,), (0,)), ((), ()))
SCALE = 1.0 / math.sqrt(T)


def collect(plan, full, pieces, behind, ahead, every):
    gather_row(full, pieces)
    full[pl.ds(ROWBLK, FIN)] = behind[...]
    full[pl.ds(ROWBLK + FIN, FIN)] = ahead[...]
    every[0] = full[plan[ME + BEFORE]]
    every[pl.ds(1, NB)] = pieces[0][...]
    every[NB + 1] = full[plan[ME + AFTER]]

    def one(k):
        every[NB + 2 + k] = full[plan[ME + k]]

    loop(RAND + GLOBALS, one)


def slots(every, i):
    spans = (
        (i, 3),
        (NB + 2 + RAND, GLOBALS),
        (NB + 2 + RANDOMS * i, RANDOMS),
    )
    return [every[pl.ds(s, n)].reshape(n * T, T) for s, n in spans]


def put_term(plan, back, k, v):
    at = plan[ME + k]
    back[jnp.where(at < ROWBLK, 2 * FIN + k, at - ROWBLK)] = v


def add_terms(plan, i, terms, rows, acc, glob, back):
    w, g, r = [jnp.dot(t, rows, preferred_element_type=F32).reshape(-1, T, T) for t in terms]
    acc[pl.ds(i, 3)] += w
    glob[...] += g
    r = r.astype(BF)
    for c in range(RANDOMS):
        put_term(plan, back, RANDOMS * i + c, r[c])


def finish(plan, acc, glob, back, grad, behind, ahead, local):
    for c in range(GLOBALS):
        put_term(plan, back, RAND + c, glob[c].astype(BF))
    put_term(plan, back, BEFORE, acc[0].astype(BF))
    put_term(plan, back, AFTER, acc[NB + 1].astype(BF))
    grad[...] = acc[pl.ds(1, NB)]
    behind[...] = back[pl.ds(0, FIN)]
    ahead[...] = back[pl.ds(FIN, FIN)]
    local[...] = back[pl.ds(2 * FIN, REQ)]


def probs_kernel(plan, q, u, *refs):
    pieces, (behind, ahead) = refs[:NZ], refs[NZ : NZ + 2]
    probs_out, every, grad, tb, ta, tl, full, acc, glob, back, held, sems = refs[NZ + 2 :]
    at = plan[ME + REQ] * NZ + plan[ME + REQ + 1]
    collect(plan, full, pieces, behind, ahead, every)
    acc[...] = jnp.zeros_like(acc)
    glob[...] = jnp.zeros_like(glob)

    def save(i):
        return pltpu.make_async_copy(held.at[i], probs_out.at[i], sems.at[i])

    def block(i):
        qi, ui = q[i], u[i]
        no_before = jnp.where((at == 0) & (i == 0), -1e30, 0.0)
        no_after = jnp.where((at == NY * NZ - 1) & (i == NB - 1), -1e30, 0.0)
        logits = [
            lax.dot_general(k, qi, NT, preferred_element_type=F32) * (SCALE * math.log2(math.e))
            for k in slots(every, i)
        ]
        window = logits[0]
        logits[0] = jnp.concatenate(
            [window[:T] + no_before, window[T : 2 * T], window[2 * T :] + no_after], axis=0
        )
        top = logits[0].max(axis=0, keepdims=True)
        for x in logits[1:]:
            top = jnp.maximum(top, x.max(axis=0, keepdims=True))
        weights = [jnp.exp2(x - top) for x in logits]
        total = sum(w.sum(axis=0, keepdims=True) for w in weights)
        inverse = 1.0 / total
        probs = [w * inverse for w in weights]
        row = 0
        for p in probs:
            held[i, pl.ds(row, p.shape[0])] = p
            row += p.shape[0]
        save(i).start()
        add_terms(plan, i, [p.astype(BF) for p in probs], ui, acc, glob, back)

    loop(NB, block)
    finish(plan, acc, glob, back, grad, tb, ta, tl)
    loop(NB, lambda i: save(i).wait())


def scores_kernel(plan, q, u, probs_in, *refs):
    pieces, (behind, ahead) = refs[:NZ], refs[NZ : NZ + 2]
    ds_out, grad, tb, ta, tl, full, values, acc, glob, back, held, low, sems, sent = refs[NZ + 2 :]

    def fetch(i):
        return pltpu.make_async_copy(probs_in.at[i], held.at[i], sems.at[i])

    def save(i):
        return pltpu.make_async_copy(low.at[i], ds_out.at[i], sent.at[i])

    loop(NB, lambda i: fetch(i).start())
    collect(plan, full, pieces, behind, ahead, values)
    acc[...] = jnp.zeros_like(acc)
    glob[...] = jnp.zeros_like(glob)

    def block(i):
        qi, ui = q[i], u[i]
        gp = [
            lax.dot_general(v, ui, NT, preferred_element_type=F32) for v in slots(values, i)
        ]
        fetch(i).wait()
        probs, row = [], 0
        for g in gp:
            probs.append(held[i, pl.ds(row, g.shape[0])])
            row += g.shape[0]
        delta = sum(
            (p.astype(BF).astype(F32) * g).sum(axis=0, keepdims=True) for p, g in zip(probs, gp)
        )
        ds = [(p * (g - delta) * SCALE).astype(BF) for p, g in zip(probs, gp)]
        row = 0
        for d in ds:
            low[i, pl.ds(row, d.shape[0])] = d
            row += d.shape[0]
        save(i).start()
        add_terms(plan, i, ds, qi, acc, glob, back)

    loop(NB, block)
    finish(plan, acc, glob, back, grad, tb, ta, tl)
    loop(NB, lambda i: save(i).wait())


def queries_kernel(ds, every, dq):
    def block(i):
        row, total = 0, None
        for k in slots(every, i):
            d = ds[i, pl.ds(row, k.shape[0])]
            part = lax.dot_general(d, k, TN, preferred_element_type=F32)
            total = part if total is None else total + part
            row += k.shape[0]
        dq[i] = total

    loop(NB, block)


def return_kernel(plan, got_up, got_down, to_down, to_up):
    for base, got, out in ((FU, got_up, to_down), (FD, got_down, to_up)):

        def one(j):
            src = plan[base + j]

            @pl.when(src >= ROWBLK)
            def _():
                out[src - ROWBLK] = got[j]

        loop(FIN, one)


def total_kernel(plan, local, got_up, got_down, far_up, far_down, *refs):
    outs, acc = refs[:NZ], refs[NZ]
    acc[...] = jnp.zeros_like(acc)
    for base, n, got in (
        (ME, REQ, local),
        (FU, FIN, got_up),
        (FD, FIN, got_down),
        (RU, REL, far_up),
        (RD, REL, far_down),
    ):

        def one(j):
            src = plan[base + j]

            @pl.when((src >= 0) & (src < ROWBLK))
            def _():
                acc[src] += got[j].astype(F32)

        loop(n, one)
    for r, out in enumerate(outs):
        out[...] = acc[pl.ds(r * NB, NB)].astype(BF)


def after(x, *earlier):
    return lax.optimization_barrier((x,) + earlier)[0]


def per_device(queries, keys, values, grad_out, out_weight, random_blocks, global_blocks):
    position = lax.axis_index("seq")
    here = [(i, i // NZ, i % NZ) for i in range(NY * NZ)]

    def along_z(x, step):
        return lax.ppermute(x, "seq", [(i, y * NZ + (z + step) % NZ) for i, y, z in here])

    def along_y(x, step):
        return lax.ppermute(x, "seq", [(i, (y + step) % NY * NZ + z) for i, y, z in here])

    q = queries.reshape(NB, T, T)

    column = lax.dynamic_index_in_dim(
        random_blocks.reshape(NY, NZ, RAND), position % NZ, 1, keepdims=False
    )
    first = (jnp.arange(NY) * NZ + position % NZ)[:, None] * NB
    edges = jnp.concatenate(
        [jnp.maximum(first - 1, 0), jnp.minimum(first + NB, NY * NZ * NB - 1)], axis=1
    )
    table = jnp.concatenate(
        [column, jnp.broadcast_to(global_blocks[None], (NY, GLOBALS)), edges], axis=1
    ).reshape(-1)
    table = jnp.concatenate([table, jnp.stack([position // NZ, position % NZ])])
    plan = call(
        plan_kernel, jax.ShapeDtypeStruct((PLAN,), jnp.int32), [SMEM], smem_out=True, moved=2000
    )(table)

    upstream = lax.dot_general(
        lax.all_gather(grad_out, "head", axis=1, tiled=True),
        out_weight,
        (((1,), (1,)), ((), ())),
        preferred_element_type=F32,
    ).astype(BF).reshape(NB, T, T)

    def pack(row):
        return call(
            pack_kernel,
            (blocks(REL), blocks(REL), blocks(FIN), blocks(FIN)),
            [SMEM] + [VMEM] * NZ,
            scratch=[pltpu.VMEM((ROWBLK, T, T), BF)],
            moved=4 << 20,
        )(plan, *row)

    def spread(ru, rd, fu, fd):
        far = along_y(ru, 1), along_y(rd, -1)
        fu, fd = call(
            relay_kernel, (blocks(FIN), blocks(FIN)), [SMEM] + [VMEM] * 4, moved=3 << 20
        )(plan, *far, fu, fd)
        return (along_y(fu, 1), along_y(fd, -1)), fu

    def hop_back(behind, ahead, *earlier):
        return along_y(after(behind, *earlier), -1), along_y(after(ahead, *earlier), 1)

    def relay_back(got_up, got_down, *earlier):
        to_down, to_up = call(
            return_kernel, (blocks(REL), blocks(REL)), [SMEM, VMEM, VMEM], moved=2 << 20
        )(plan, after(got_up, *earlier), got_down)
        return (along_y(to_down, -1), along_y(to_up, 1)), to_down

    def add_up(local, got_up, got_down, far_up, far_down):
        return call(
            total_kernel,
            (blocks(NB),) * NZ,
            [SMEM] + [VMEM] * 5,
            scratch=[pltpu.VMEM((ROWBLK, T, T), F32)],
            moved=5 << 20,
        )(plan, local, got_up, got_down, far_up, far_down)

    def ring_start(parts, plus, minus):
        return [(parts, 1, plus, along_z(parts[plus], 1))] + [
            (parts, -1, minus, along_z(parts[NZ - minus], -1))
        ]

    def ring_next(rings):
        sums = [
            (moving.astype(F32) + parts[step * (left - 1) % NZ].astype(F32)).astype(BF)
            for parts, step, left, moving in rings
        ]
        return [
            (parts, step, left - 1, along_z(x, step))
            for (parts, step, left, _), x in zip(rings, sums)
        ]

    def ring_end(grad, rings):
        while any(left > 1 for _, _, left, _ in rings):
            more = [r for r in rings if r[2] > 1]
            rings = [r for r in rings if r[2] == 1] + ring_next(more)
        out = grad + rings[0][0][0].astype(F32) + sum(r[3].astype(F32) for r in rings)
        return out.reshape(NB * T, T)

    scratch = [
        pltpu.VMEM((NB + 2, T, T), F32),
        pltpu.VMEM((GLOBALS, T, T), F32),
        pltpu.VMEM((2 * FIN + REQ, T, T), BF),
        pltpu.VMEM((NB, 8 * T, T), F32),
        pltpu.SemaphoreType.DMA((NB,)),
    ]
    full = pltpu.VMEM((ROWBLK + 2 * FIN, T, T), BF)
    every = NB + 2 + RAND + GLOBALS
    grads = (blocks(NB, F32), blocks(FIN), blocks(FIN), blocks(REQ))
    anywhere = pl.BlockSpec(memory_space=pl.ANY)

    krow = [keys.reshape(NB, T, T)] + [None] * (NZ - 1)
    vrow = [values.reshape(NB, T, T)] + [None] * (NZ - 1)

    def step(row, s, *earlier, plus=True, minus=True):
        up, down = row[(NZ + 1 - s) % NZ], row[s - 1]
        if plus:
            row[NZ - s] = along_z(after(up, *earlier) if earlier else up, 1)
        if minus:
            row[s] = along_z(after(down, *earlier) if earlier else down, -1)

    step(krow, 1)
    step(vrow, 1)
    step(krow, 2)
    step(vrow, 2)
    step(krow, 3, plan)
    step(vrow, 3)
    step(krow, 4, minus=False)
    step(vrow, 4, plus=False)
    kpack = pack(krow)
    vpack = pack(vrow)
    kfin, _ = spread(*kpack)
    vfin, vready = spread(*vpack)

    probs, kall, gv, *vback = call(
        probs_kernel,
        (jax.ShapeDtypeStruct((NB, 8 * T, T), F32), blocks(every)) + grads,
        [SMEM] + [VMEM] * (2 + NZ + 2),
        outs_at=[anywhere] + [VMEM] * 5,
        scratch=[full] + scratch,
        flops=2 * 2 * 64 * T**3,
        moved=12 << 20,
        limit=48,
    )(plan, after(q, vready), upstream, *krow, *kfin)
    ds, gk, *kback = call(
        scores_kernel,
        (jax.ShapeDtypeStruct((NB, 8 * T, T), BF),) + grads,
        [SMEM] + [VMEM] * 2 + [anywhere] + [VMEM] * (NZ + 2),
        outs_at=[anywhere] + [VMEM] * 4,
        scratch=[full, pltpu.VMEM((every, T, T), BF)]
        + scratch[:-1]
        + [pltpu.VMEM((NB, 8 * T, T), BF)]
        + [scratch[-1]] * 2,
        flops=2 * 3 * 64 * T**3,
        moved=12 << 20,
        limit=48,
    )(plan, q, upstream, probs, *vrow, *vfin)

    vgot = hop_back(*vback[:2])
    vfar, vsent = relay_back(*vgot, kback[0])
    kgot = hop_back(*kback[:2], vsent)
    dq = call(
        queries_kernel, blocks(NB, F32), [VMEM, VMEM], flops=2 * 64 * T**3, moved=4 << 20
    )(after(ds, vsent), kall)
    kfar, ksent = relay_back(*kgot, dq)
    vparts = add_up(after(vback[2], ksent), *vgot, *vfar)
    vring = ring_start(vparts, 3, 4)
    kring = ring_start(add_up(kback[2], *kgot, *kfar), 4, 3)
    dv = ring_end(gv, vring)
    dk = ring_end(gk, kring)
    return dq.reshape(NB * T, T), dk, dv


def solution(mesh):
    return jax.shard_map(
        per_device,
        mesh=mesh,
        in_specs=(P("seq", "head"),) * 4 + (P("head", None), P(), P()),
        out_specs=(P("seq", "head"),) * 3,
        check_vma=False,
    )
```

```python
import math

import jax
import jax.numpy as jnp
from jax import lax
from jax.experimental import pallas as pl
from jax.experimental.pallas import tpu as pltpu
from jax.sharding import PartitionSpec as P

T = 128
GLOBALS = 2
RANDOMS = 3
NB = 8
NY = 4
NZ = 8
RAND = NB * RANDOMS
REQ = RAND + GLOBALS + 2
BEFORE, AFTER = REQ - 2, REQ - 1
ROWBLK = NZ * NB
FIN = 19
REL = 9

RU, RD = 0, REL
FU, FD = 2 * REL, 2 * REL + FIN
ME = 2 * REL + 2 * FIN
PLAN = ME + REQ + 2

BF = jnp.bfloat16
F32 = jnp.float32
VMEM = pl.BlockSpec(memory_space=pltpu.VMEM)
SMEM = pl.BlockSpec(memory_space=pltpu.SMEM)


def call(kernel, outs, ins, scratch=(), smem_out=False, outs_at=None, flops=0, moved=0, limit=48):
    return pl.pallas_call(
        kernel,
        out_shape=outs,
        in_specs=ins,
        out_specs=outs_at or jax.tree.map(lambda _: SMEM if smem_out else VMEM, outs),
        scratch_shapes=list(scratch),
        cost_estimate=pl.CostEstimate(flops=flops, bytes_accessed=moved, transcendentals=0),
        compiler_params=pltpu.CompilerParams(vmem_limit_bytes=limit * 1024 * 1024),
    )


def blocks(n, dtype=BF):
    return jax.ShapeDtypeStruct((n, T, T), dtype)


def plan_kernel(tab, plan):
    y, z = tab[NY * REQ], tab[NY * REQ + 1]

    def clear(j, c):
        plan[j] = -1
        return c

    lax.fori_loop(0, ME, clear, 0, unroll=8)
    plan[ME + REQ] = y
    plan[ME + REQ + 1] = z
    for off in range(NY):
        yd = (y + off) & (NY - 1)

        def where(k):
            b = tab[yd * REQ + k]
            far = ((b >> 6) - yd) & (NY - 1)
            return far, ((((b >> 3) - z) & (NZ - 1)) << 3) | (b & 7)

        def count(k, c):
            far, _ = where(k)
            return tuple(n + (far == r).astype(jnp.int32) for n, r in zip(c, (1, 2, 3)))

        zero = jnp.int32(0)
        ahead, across, behind = lax.fori_loop(
            0, REQ, count, (zero, zero, zero), unroll=7
        )
        low = jnp.maximum(jnp.maximum(across - REL, ahead + across - FIN), 0)
        high = jnp.minimum(jnp.minimum(across, REL), FIN - behind)
        via = jnp.minimum(jnp.maximum(across >> 1, low), high)

        def place(k, c):
            used_ahead, used_across, used_behind = c
            far, src = where(k)
            is1, is2, is3 = far == 1, far == 2, far == 3
            first = used_across < via
            down_slot = jnp.where(is3, used_behind, behind + used_across)
            up_slot = jnp.where(is1, used_ahead, ahead + used_across - via)
            from_behind = is3 | (is2 & first)
            from_ahead = is1 | (is2 & jnp.logical_not(first))
            if off == 0:
                plan[ME + k] = jnp.where(
                    from_behind,
                    ROWBLK + down_slot,
                    jnp.where(from_ahead, ROWBLK + FIN + up_slot, src),
                )
            elif off == 1:

                @pl.when(from_behind)
                def _():
                    plan[FU + down_slot] = jnp.where(is3, src, ROWBLK + used_across)
            elif off == 3:

                @pl.when(from_ahead)
                def _():
                    plan[FD + up_slot] = jnp.where(is1, src, ROWBLK + used_across - via)
            else:

                @pl.when(is2)
                def _():
                    plan[jnp.where(first, RU + used_across, RD + used_across - via)] = src

            return (
                used_ahead + is1.astype(jnp.int32),
                used_across + is2.astype(jnp.int32),
                used_behind + is3.astype(jnp.int32),
            )

        lax.fori_loop(0, REQ, place, (zero, zero, zero), unroll=4)


def loop(n, body):
    def step(j, c):
        body(j)
        return c

    lax.fori_loop(0, n, step, 0)


def gather_row(full, pieces):
    for r, piece in enumerate(pieces):
        full[pl.ds(r * NB, NB)] = piece[...]


def pack_kernel(plan, *refs):
    pieces, (ru, rd, fu, fd, full) = refs[:NZ], refs[NZ:]
    gather_row(full, pieces)
    for base, n, out in ((RU, REL, ru), (RD, REL, rd), (FU, FIN, fu), (FD, FIN, fd)):

        def one(j):
            src = plan[base + j]
            out[j] = full[jnp.where((src < 0) | (src >= ROWBLK), 0, src)]

        loop(n, one)


def relay_kernel(plan, got_up, got_down, fu_in, fd_in, fu, fd):
    for base, got, into, out in ((FU, got_up, fu_in, fu), (FD, got_down, fd_in, fd)):
        out[...] = into[...]

        def one(j):
            src = plan[base + j]

            @pl.when(src >= ROWBLK)
            def _():
                out[j] = got[src - ROWBLK]

        loop(FIN, one)


NT = (((1,), (1,)), ((), ()))
TN = (((0,), (0,)), ((), ()))
SCALE = 1.0 / math.sqrt(T)


def collect(plan, full, pieces, behind, ahead, every):
    gather_row(full, pieces)
    full[pl.ds(ROWBLK, FIN)] = behind[...]
    full[pl.ds(ROWBLK + FIN, FIN)] = ahead[...]
    every[0] = full[plan[ME + BEFORE]]
    every[pl.ds(1, NB)] = pieces[0][...]
    every[NB + 1] = full[plan[ME + AFTER]]

    def one(k):
        every[NB + 2 + k] = full[plan[ME + k]]

    loop(RAND + GLOBALS, one)


def slots(every, i):
    spans = (
        (i, 3),
        (NB + 2 + RAND, GLOBALS),
        (NB + 2 + RANDOMS * i, RANDOMS),
    )
    return [every[pl.ds(s, n)].reshape(n * T, T) for s, n in spans]


def put_term(plan, back, k, v):
    at = plan[ME + k]
    back[jnp.where(at < ROWBLK, 2 * FIN + k, at - ROWBLK)] = v


def add_terms(plan, i, terms, rows, acc, glob, back):
    w, g, r = [jnp.dot(t, rows, preferred_element_type=F32).reshape(-1, T, T) for t in terms]
    acc[pl.ds(i, 3)] += w
    glob[...] += g
    r = r.astype(BF)
    for c in range(RANDOMS):
        put_term(plan, back, RANDOMS * i + c, r[c])


def finish(plan, acc, glob, back, grad, behind, ahead, local):
    for c in range(GLOBALS):
        put_term(plan, back, RAND + c, glob[c].astype(BF))
    put_term(plan, back, BEFORE, acc[0].astype(BF))
    put_term(plan, back, AFTER, acc[NB + 1].astype(BF))
    grad[...] = acc[pl.ds(1, NB)]
    behind[...] = back[pl.ds(0, FIN)]
    ahead[...] = back[pl.ds(FIN, FIN)]
    local[...] = back[pl.ds(2 * FIN, REQ)]


def probs_kernel(plan, q, u, *refs):
    pieces, (behind, ahead) = refs[:NZ], refs[NZ : NZ + 2]
    probs_out, every, grad, tb, ta, tl, full, acc, glob, back, held, sems = refs[NZ + 2 :]
    at = plan[ME + REQ] * NZ + plan[ME + REQ + 1]
    collect(plan, full, pieces, behind, ahead, every)
    acc[...] = jnp.zeros_like(acc)
    glob[...] = jnp.zeros_like(glob)

    def save(i):
        return pltpu.make_async_copy(held.at[i], probs_out.at[i], sems.at[i])

    def block(i):
        qi, ui = q[i], u[i]
        no_before = jnp.where((at == 0) & (i == 0), -1e30, 0.0)
        no_after = jnp.where((at == NY * NZ - 1) & (i == NB - 1), -1e30, 0.0)
        logits = [
            lax.dot_general(k, qi, NT, preferred_element_type=F32) * (SCALE * math.log2(math.e))
            for k in slots(every, i)
        ]
        window = logits[0]
        logits[0] = jnp.concatenate(
            [window[:T] + no_before, window[T : 2 * T], window[2 * T :] + no_after], axis=0
        )
        top = logits[0].max(axis=0, keepdims=True)
        for x in logits[1:]:
            top = jnp.maximum(top, x.max(axis=0, keepdims=True))
        weights = [jnp.exp2(x - top) for x in logits]
        total = sum(w.sum(axis=0, keepdims=True) for w in weights)
        inverse = 1.0 / total
        probs = [w * inverse for w in weights]
        row = 0
        for p in probs:
            held[i, pl.ds(row, p.shape[0])] = p
            row += p.shape[0]
        save(i).start()
        add_terms(plan, i, [p.astype(BF) for p in probs], ui, acc, glob, back)

    loop(NB, block)
    finish(plan, acc, glob, back, grad, tb, ta, tl)
    loop(NB, lambda i: save(i).wait())


def scores_kernel(plan, q, u, probs_in, *refs):
    pieces, (behind, ahead) = refs[:NZ], refs[NZ : NZ + 2]
    ds_out, grad, tb, ta, tl, full, values, acc, glob, back, held, low, sems, sent = refs[NZ + 2 :]

    def fetch(i):
        return pltpu.make_async_copy(probs_in.at[i], held.at[i], sems.at[i])

    def save(i):
        return pltpu.make_async_copy(low.at[i], ds_out.at[i], sent.at[i])

    loop(NB, lambda i: fetch(i).start())
    collect(plan, full, pieces, behind, ahead, values)
    acc[...] = jnp.zeros_like(acc)
    glob[...] = jnp.zeros_like(glob)

    def block(i):
        qi, ui = q[i], u[i]
        gp = [
            lax.dot_general(v, ui, NT, preferred_element_type=F32) for v in slots(values, i)
        ]
        fetch(i).wait()
        probs, row = [], 0
        for g in gp:
            probs.append(held[i, pl.ds(row, g.shape[0])])
            row += g.shape[0]
        delta = sum(
            (p.astype(BF).astype(F32) * g).sum(axis=0, keepdims=True) for p, g in zip(probs, gp)
        )
        ds = [(p * (g - delta) * SCALE).astype(BF) for p, g in zip(probs, gp)]
        row = 0
        for d in ds:
            low[i, pl.ds(row, d.shape[0])] = d
            row += d.shape[0]
        save(i).start()
        add_terms(plan, i, ds, qi, acc, glob, back)

    loop(NB, block)
    finish(plan, acc, glob, back, grad, tb, ta, tl)
    loop(NB, lambda i: save(i).wait())


def queries_kernel(ds, every, dq):
    def block(i):
        row, total = 0, None
        for k in slots(every, i):
            d = ds[i, pl.ds(row, k.shape[0])]
            part = lax.dot_general(d, k, TN, preferred_element_type=F32)
            total = part if total is None else total + part
            row += k.shape[0]
        dq[i] = total

    loop(NB, block)


def return_kernel(plan, got_up, got_down, to_down, to_up):
    for base, got, out in ((FU, got_up, to_down), (FD, got_down, to_up)):

        def one(j):
            src = plan[base + j]

            @pl.when(src >= ROWBLK)
            def _():
                out[src - ROWBLK] = got[j]

        loop(FIN, one)


def total_kernel(plan, local, got_up, got_down, far_up, far_down, *refs):
    outs, acc = refs[:NZ], refs[NZ]
    acc[...] = jnp.zeros_like(acc)
    for base, n, got in (
        (ME, REQ, local),
        (FU, FIN, got_up),
        (FD, FIN, got_down),
        (RU, REL, far_up),
        (RD, REL, far_down),
    ):

        def one(j):
            src = plan[base + j]

            @pl.when((src >= 0) & (src < ROWBLK))
            def _():
                acc[src] += got[j].astype(F32)

        loop(n, one)
    for r, out in enumerate(outs):
        out[...] = acc[pl.ds(r * NB, NB)].astype(BF)


def after(x, *earlier):
    return lax.optimization_barrier((x,) + earlier)[0]


def per_device(queries, keys, values, grad_out, out_weight, random_blocks, global_blocks):
    position = lax.axis_index("seq")
    here = [(i, i // NZ, i % NZ) for i in range(NY * NZ)]

    def along_z(x, step):
        return lax.ppermute(x, "seq", [(i, y * NZ + (z + step) % NZ) for i, y, z in here])

    def along_y(x, step):
        return lax.ppermute(x, "seq", [(i, (y + step) % NY * NZ + z) for i, y, z in here])

    q = queries.reshape(NB, T, T)

    column = lax.dynamic_index_in_dim(
        random_blocks.reshape(NY, NZ, RAND), position % NZ, 1, keepdims=False
    )
    first = (jnp.arange(NY) * NZ + position % NZ)[:, None] * NB
    edges = jnp.concatenate(
        [jnp.maximum(first - 1, 0), jnp.minimum(first + NB, NY * NZ * NB - 1)], axis=1
    )
    table = jnp.concatenate(
        [column, jnp.broadcast_to(global_blocks[None], (NY, GLOBALS)), edges], axis=1
    ).reshape(-1)
    table = jnp.concatenate([table, jnp.stack([position // NZ, position % NZ])])
    plan = call(
        plan_kernel, jax.ShapeDtypeStruct((PLAN,), jnp.int32), [SMEM], smem_out=True, moved=2000
    )(table)

    upstream = lax.dot_general(
        lax.all_gather(grad_out, "head", axis=1, tiled=True),
        out_weight,
        (((1,), (1,)), ((), ())),
        preferred_element_type=F32,
    ).astype(BF).reshape(NB, T, T)

    def pack(row):
        return call(
            pack_kernel,
            (blocks(REL), blocks(REL), blocks(FIN), blocks(FIN)),
            [SMEM] + [VMEM] * NZ,
            scratch=[pltpu.VMEM((ROWBLK, T, T), BF)],
            moved=4 << 20,
        )(plan, *row)

    def spread(ru, rd, fu, fd):
        far = along_y(ru, 1), along_y(rd, -1)
        fu, fd = call(
            relay_kernel, (blocks(FIN), blocks(FIN)), [SMEM] + [VMEM] * 4, moved=3 << 20
        )(plan, *far, fu, fd)
        return (along_y(fu, 1), along_y(fd, -1)), fu

    def hop_back(behind, ahead, *earlier):
        return along_y(after(behind, *earlier), -1), along_y(after(ahead, *earlier), 1)

    def relay_back(got_up, got_down, *earlier):
        to_down, to_up = call(
            return_kernel, (blocks(REL), blocks(REL)), [SMEM, VMEM, VMEM], moved=2 << 20
        )(plan, after(got_up, *earlier), got_down)
        return (along_y(to_down, -1), along_y(to_up, 1)), to_down

    def add_up(local, got_up, got_down, far_up, far_down):
        return call(
            total_kernel,
            (blocks(NB),) * NZ,
            [SMEM] + [VMEM] * 5,
            scratch=[pltpu.VMEM((ROWBLK, T, T), F32)],
            moved=5 << 20,
        )(plan, local, got_up, got_down, far_up, far_down)

    def ring_start(parts, plus, minus):
        return [(parts, 1, plus, along_z(parts[plus], 1))] + [
            (parts, -1, minus, along_z(parts[NZ - minus], -1))
        ]

    def ring_next(rings):
        sums = [
            (moving.astype(F32) + parts[step * (left - 1) % NZ].astype(F32)).astype(BF)
            for parts, step, left, moving in rings
        ]
        return [
            (parts, step, left - 1, along_z(x, step))
            for (parts, step, left, _), x in zip(rings, sums)
        ]

    def ring_end(grad, rings):
        while any(left > 1 for _, _, left, _ in rings):
            more = [r for r in rings if r[2] > 1]
            rings = [r for r in rings if r[2] == 1] + ring_next(more)
        out = grad + rings[0][0][0].astype(F32) + sum(r[3].astype(F32) for r in rings)
        return out.reshape(NB * T, T)

    scratch = [
        pltpu.VMEM((NB + 2, T, T), F32),
        pltpu.VMEM((GLOBALS, T, T), F32),
        pltpu.VMEM((2 * FIN + REQ, T, T), BF),
        pltpu.VMEM((NB, 8 * T, T), F32),
        pltpu.SemaphoreType.DMA((NB,)),
    ]
    full = pltpu.VMEM((ROWBLK + 2 * FIN, T, T), BF)
    every = NB + 2 + RAND + GLOBALS
    grads = (blocks(NB, F32), blocks(FIN), blocks(FIN), blocks(REQ))
    anywhere = pl.BlockSpec(memory_space=pl.ANY)

    krow = [keys.reshape(NB, T, T)] + [None] * (NZ - 1)
    vrow = [values.reshape(NB, T, T)] + [None] * (NZ - 1)

    def step(row, s, *earlier, plus=True, minus=True):
        up, down = row[(NZ + 1 - s) % NZ], row[s - 1]
        if plus:
            row[NZ - s] = along_z(after(up, *earlier) if earlier else up, 1)
        if minus:
            row[s] = along_z(after(down, *earlier) if earlier else down, -1)

    step(krow, 1)
    step(vrow, 1)
    step(krow, 2)
    step(vrow, 2)
    step(krow, 3, plan)
    step(vrow, 3)
    step(krow, 4, minus=False)
    step(vrow, 4, plus=False)
    kpack = pack(krow)
    vpack = pack(vrow)
    kfin, _ = spread(*kpack)
    vfin, vready = spread(*vpack)

    probs, kall, gv, *vback = call(
        probs_kernel,
        (jax.ShapeDtypeStruct((NB, 8 * T, T), F32), blocks(every)) + grads,
        [SMEM] + [VMEM] * (2 + NZ + 2),
        outs_at=[anywhere] + [VMEM] * 5,
        scratch=[full] + scratch,
        flops=2 * 2 * 64 * T**3,
        moved=12 << 20,
        limit=48,
    )(plan, after(q, vready), upstream, *krow, *kfin)
    ds, gk, *kback = call(
        scores_kernel,
        (jax.ShapeDtypeStruct((NB, 8 * T, T), BF),) + grads,
        [SMEM] + [VMEM] * 2 + [anywhere] + [VMEM] * (NZ + 2),
        outs_at=[anywhere] + [VMEM] * 4,
        scratch=[full, pltpu.VMEM((every, T, T), BF)]
        + scratch[:-1]
        + [pltpu.VMEM((NB, 8 * T, T), BF)]
        + [scratch[-1]] * 2,
        flops=2 * 3 * 64 * T**3,
        moved=12 << 20,
        limit=48,
    )(plan, q, upstream, probs, *vrow, *vfin)

    vgot = hop_back(*vback[:2])
    vfar, vsent = relay_back(*vgot, kback[0])
    kgot = hop_back(*kback[:2], vsent)
    dq = call(
        queries_kernel, blocks(NB, F32), [VMEM, VMEM], flops=2 * 64 * T**3, moved=4 << 20
    )(after(ds, vsent), kall)
    kfar, ksent = relay_back(*kgot, dq)
    vparts = add_up(after(vback[2], ksent), *vgot, *vfar)
    vring = ring_start(vparts, 3, 4)
    kring = ring_start(add_up(kback[2], *kgot, *kfar), 4, 3)
    dv = ring_end(gv, vring)
    dk = ring_end(gk, kring)
    return dq.reshape(NB * T, T), dk, dv


def solution(mesh):
    return jax.shard_map(
        per_device,
        mesh=mesh,
        in_specs=(P("seq", "head"),) * 4 + (P("head", None), P(), P()),
        out_specs=(P("seq", "head"),) * 3,
        check_vma=False,
    )
```

```python
import math

import jax
import jax.numpy as jnp
from jax import lax
from jax.experimental import pallas as pl
from jax.experimental.pallas import tpu as pltpu
from jax.sharding import PartitionSpec as P

T = 128
GLOBALS = 2
RANDOMS = 3
NB = 8
NY = 4
NZ = 8
RAND = NB * RANDOMS
REQ = RAND + GLOBALS + 2
BEFORE, AFTER = REQ - 2, REQ - 1
ROWBLK = NZ * NB
FIN = 19
REL = 9

RU, RD = 0, REL
FU, FD = 2 * REL, 2 * REL + FIN
ME = 2 * REL + 2 * FIN
PLAN = ME + REQ + 2

BF = jnp.bfloat16
F32 = jnp.float32
VMEM = pl.BlockSpec(memory_space=pltpu.VMEM)
SMEM = pl.BlockSpec(memory_space=pltpu.SMEM)


def call(kernel, outs, ins, scratch=(), smem_out=False, outs_at=None, flops=0, moved=0, limit=48):
    return pl.pallas_call(
        kernel,
        out_shape=outs,
        in_specs=ins,
        out_specs=outs_at or jax.tree.map(lambda _: SMEM if smem_out else VMEM, outs),
        scratch_shapes=list(scratch),
        cost_estimate=pl.CostEstimate(flops=flops, bytes_accessed=moved, transcendentals=0),
        compiler_params=pltpu.CompilerParams(vmem_limit_bytes=limit * 1024 * 1024),
    )


def blocks(n, dtype=BF):
    return jax.ShapeDtypeStruct((n, T, T), dtype)


def plan_kernel(tab, plan):
    y, z = tab[NY * REQ], tab[NY * REQ + 1]

    def clear(j, c):
        plan[j] = -1
        return c

    lax.fori_loop(0, ME, clear, 0, unroll=8)
    plan[ME + REQ] = y
    plan[ME + REQ + 1] = z
    for off in range(NY):
        yd = (y + off) & (NY - 1)

        def where(k):
            b = tab[yd * REQ + k]
            far = ((b >> 6) - yd) & (NY - 1)
            return far, ((((b >> 3) - z) & (NZ - 1)) << 3) | (b & 7)

        def count(k, c):
            far, _ = where(k)
            return tuple(n + (far == r).astype(jnp.int32) for n, r in zip(c, (1, 2, 3)))

        zero = jnp.int32(0)
        ahead, across, behind = lax.fori_loop(
            0, REQ, count, (zero, zero, zero), unroll=7
        )
        low = jnp.maximum(jnp.maximum(across - REL, ahead + across - FIN), 0)
        high = jnp.minimum(jnp.minimum(across, REL), FIN - behind)
        via = jnp.minimum(jnp.maximum(across >> 1, low), high)

        def place(k, c):
            used_ahead, used_across, used_behind = c
            far, src = where(k)
            is1, is2, is3 = far == 1, far == 2, far == 3
            first = used_across < via
            down_slot = jnp.where(is3, used_behind, behind + used_across)
            up_slot = jnp.where(is1, used_ahead, ahead + used_across - via)
            from_behind = is3 | (is2 & first)
            from_ahead = is1 | (is2 & jnp.logical_not(first))
            if off == 0:
                plan[ME + k] = jnp.where(
                    from_behind,
                    ROWBLK + down_slot,
                    jnp.where(from_ahead, ROWBLK + FIN + up_slot, src),
                )
            elif off == 1:

                @pl.when(from_behind)
                def _():
                    plan[FU + down_slot] = jnp.where(is3, src, ROWBLK + used_across)
            elif off == 3:

                @pl.when(from_ahead)
                def _():
                    plan[FD + up_slot] = jnp.where(is1, src, ROWBLK + used_across - via)
            else:

                @pl.when(is2)
                def _():
                    plan[jnp.where(first, RU + used_across, RD + used_across - via)] = src

            return (
                used_ahead + is1.astype(jnp.int32),
                used_across + is2.astype(jnp.int32),
                used_behind + is3.astype(jnp.int32),
            )

        lax.fori_loop(0, REQ, place, (zero, zero, zero), unroll=4)


def loop(n, body):
    def step(j, c):
        body(j)
        return c

    lax.fori_loop(0, n, step, 0)


def gather_row(full, pieces):
    for r, piece in enumerate(pieces):
        full[pl.ds(r * NB, NB)] = piece[...]


def pack_kernel(plan, *refs):
    pieces, (ru, rd, fu, fd, full) = refs[:NZ], refs[NZ:]
    gather_row(full, pieces)
    for base, n, out in ((RU, REL, ru), (RD, REL, rd), (FU, FIN, fu), (FD, FIN, fd)):

        def one(j):
            src = plan[base + j]
            out[j] = full[jnp.where((src < 0) | (src >= ROWBLK), 0, src)]

        loop(n, one)


def relay_kernel(plan, got_up, got_down, fu_in, fd_in, fu, fd):
    for base, got, into, out in ((FU, got_up, fu_in, fu), (FD, got_down, fd_in, fd)):
        out[...] = into[...]

        def one(j):
            src = plan[base + j]

            @pl.when(src >= ROWBLK)
            def _():
                out[j] = got[src - ROWBLK]

        loop(FIN, one)


NT = (((1,), (1,)), ((), ()))
TN = (((0,), (0,)), ((), ()))
SCALE = 1.0 / math.sqrt(T)


def collect(plan, full, pieces, behind, ahead, every):
    gather_row(full, pieces)
    full[pl.ds(ROWBLK, FIN)] = behind[...]
    full[pl.ds(ROWBLK + FIN, FIN)] = ahead[...]
    every[0] = full[plan[ME + BEFORE]]
    every[pl.ds(1, NB)] = pieces[0][...]
    every[NB + 1] = full[plan[ME + AFTER]]

    def one(k):
        every[NB + 2 + k] = full[plan[ME + k]]

    loop(RAND + GLOBALS, one)


def slots(every, i):
    spans = (
        (i, 3),
        (NB + 2 + RAND, GLOBALS),
        (NB + 2 + RANDOMS * i, RANDOMS),
    )
    return [every[pl.ds(s, n)].reshape(n * T, T) for s, n in spans]


def put_term(plan, back, k, v):
    at = plan[ME + k]
    back[jnp.where(at < ROWBLK, 2 * FIN + k, at - ROWBLK)] = v


def add_terms(plan, i, terms, rows, acc, glob, back):
    w, g, r = [jnp.dot(t, rows, preferred_element_type=F32).reshape(-1, T, T) for t in terms]
    acc[pl.ds(i, 3)] += w
    glob[...] += g
    r = r.astype(BF)
    for c in range(RANDOMS):
        put_term(plan, back, RANDOMS * i + c, r[c])


def finish(plan, acc, glob, back, grad, behind, ahead, local):
    for c in range(GLOBALS):
        put_term(plan, back, RAND + c, glob[c].astype(BF))
    put_term(plan, back, BEFORE, acc[0].astype(BF))
    put_term(plan, back, AFTER, acc[NB + 1].astype(BF))
    grad[...] = acc[pl.ds(1, NB)]
    behind[...] = back[pl.ds(0, FIN)]
    ahead[...] = back[pl.ds(FIN, FIN)]
    local[...] = back[pl.ds(2 * FIN, REQ)]


def probs_kernel(plan, q, u, *refs):
    pieces, (behind, ahead) = refs[:NZ], refs[NZ : NZ + 2]
    probs_out, every, grad, tb, ta, tl, full, acc, glob, back, held, sems = refs[NZ + 2 :]
    at = plan[ME + REQ] * NZ + plan[ME + REQ + 1]
    collect(plan, full, pieces, behind, ahead, every)
    acc[...] = jnp.zeros_like(acc)
    glob[...] = jnp.zeros_like(glob)

    def save(i):
        return pltpu.make_async_copy(held.at[i], probs_out.at[i], sems.at[i])

    def block(i):
        qi, ui = q[i], u[i]
        no_before = jnp.where((at == 0) & (i == 0), -1e30, 0.0)
        no_after = jnp.where((at == NY * NZ - 1) & (i == NB - 1), -1e30, 0.0)
        logits = [
            lax.dot_general(k, qi, NT, preferred_element_type=F32) * (SCALE * math.log2(math.e))
            for k in slots(every, i)
        ]
        window = logits[0]
        logits[0] = jnp.concatenate(
            [window[:T] + no_before, window[T : 2 * T], window[2 * T :] + no_after], axis=0
        )
        top = logits[0].max(axis=0, keepdims=True)
        for x in logits[1:]:
            top = jnp.maximum(top, x.max(axis=0, keepdims=True))
        weights = [jnp.exp2(x - top) for x in logits]
        total = sum(w.sum(axis=0, keepdims=True) for w in weights)
        inverse = 1.0 / total
        probs = [w * inverse for w in weights]
        row = 0
        for p in probs:
            held[i, pl.ds(row, p.shape[0])] = p
            row += p.shape[0]
        save(i).start()
        add_terms(plan, i, [p.astype(BF) for p in probs], ui, acc, glob, back)

    loop(NB, block)
    finish(plan, acc, glob, back, grad, tb, ta, tl)
    loop(NB, lambda i: save(i).wait())


def scores_kernel(plan, q, u, probs_in, *refs):
    pieces, (behind, ahead) = refs[:NZ], refs[NZ : NZ + 2]
    ds_out, grad, tb, ta, tl, full, values, acc, glob, back, held, low, sems, sent = refs[NZ + 2 :]

    def fetch(i):
        return pltpu.make_async_copy(probs_in.at[i], held.at[i], sems.at[i])

    def save(i):
        return pltpu.make_async_copy(low.at[i], ds_out.at[i], sent.at[i])

    loop(NB, lambda i: fetch(i).start())
    collect(plan, full, pieces, behind, ahead, values)
    acc[...] = jnp.zeros_like(acc)
    glob[...] = jnp.zeros_like(glob)

    def block(i):
        qi, ui = q[i], u[i]
        gp = [
            lax.dot_general(v, ui, NT, preferred_element_type=F32) for v in slots(values, i)
        ]
        fetch(i).wait()
        probs, row = [], 0
        for g in gp:
            probs.append(held[i, pl.ds(row, g.shape[0])])
            row += g.shape[0]
        delta = sum(
            (p.astype(BF).astype(F32) * g).sum(axis=0, keepdims=True) for p, g in zip(probs, gp)
        )
        ds = [(p * (g - delta) * SCALE).astype(BF) for p, g in zip(probs, gp)]
        row = 0
        for d in ds:
            low[i, pl.ds(row, d.shape[0])] = d
            row += d.shape[0]
        save(i).start()
        add_terms(plan, i, ds, qi, acc, glob, back)

    loop(NB, block)
    finish(plan, acc, glob, back, grad, tb, ta, tl)
    loop(NB, lambda i: save(i).wait())


def queries_kernel(ds, every, dq):
    def block(i):
        row, total = 0, None
        for k in slots(every, i):
            d = ds[i, pl.ds(row, k.shape[0])]
            part = lax.dot_general(d, k, TN, preferred_element_type=F32)
            total = part if total is None else total + part
            row += k.shape[0]
        dq[i] = total

    loop(NB, block)


def return_kernel(plan, got_up, got_down, to_down, to_up):
    for base, got, out in ((FU, got_up, to_down), (FD, got_down, to_up)):

        def one(j):
            src = plan[base + j]

            @pl.when(src >= ROWBLK)
            def _():
                out[src - ROWBLK] = got[j]

        loop(FIN, one)


def total_kernel(plan, local, got_up, got_down, far_up, far_down, *refs):
    outs, acc = refs[:NZ], refs[NZ]
    acc[...] = jnp.zeros_like(acc)
    for base, n, got in (
        (ME, REQ, local),
        (FU, FIN, got_up),
        (FD, FIN, got_down),
        (RU, REL, far_up),
        (RD, REL, far_down),
    ):

        def one(j):
            src = plan[base + j]

            @pl.when((src >= 0) & (src < ROWBLK))
            def _():
                acc[src] += got[j].astype(F32)

        loop(n, one)
    for r, out in enumerate(outs):
        out[...] = acc[pl.ds(r * NB, NB)].astype(BF)


def after(x, *earlier):
    return lax.optimization_barrier((x,) + earlier)[0]


def per_device(queries, keys, values, grad_out, out_weight, random_blocks, global_blocks):
    position = lax.axis_index("seq")
    here = [(i, i // NZ, i % NZ) for i in range(NY * NZ)]

    def along_z(x, step):
        return lax.ppermute(x, "seq", [(i, y * NZ + (z + step) % NZ) for i, y, z in here])

    def along_y(x, step):
        return lax.ppermute(x, "seq", [(i, (y + step) % NY * NZ + z) for i, y, z in here])

    q = queries.reshape(NB, T, T)

    column = lax.dynamic_index_in_dim(
        random_blocks.reshape(NY, NZ, RAND), position % NZ, 1, keepdims=False
    )
    first = (jnp.arange(NY) * NZ + position % NZ)[:, None] * NB
    edges = jnp.concatenate(
        [jnp.maximum(first - 1, 0), jnp.minimum(first + NB, NY * NZ * NB - 1)], axis=1
    )
    table = jnp.concatenate(
        [column, jnp.broadcast_to(global_blocks[None], (NY, GLOBALS)), edges], axis=1
    ).reshape(-1)
    table = jnp.concatenate([table, jnp.stack([position // NZ, position % NZ])])
    plan = call(
        plan_kernel, jax.ShapeDtypeStruct((PLAN,), jnp.int32), [SMEM], smem_out=True, moved=2000
    )(table)

    upstream = lax.dot_general(
        lax.all_gather(grad_out, "head", axis=1, tiled=True),
        out_weight,
        (((1,), (1,)), ((), ())),
        preferred_element_type=F32,
    ).astype(BF).reshape(NB, T, T)

    def pack(row):
        return call(
            pack_kernel,
            (blocks(REL), blocks(REL), blocks(FIN), blocks(FIN)),
            [SMEM] + [VMEM] * NZ,
            scratch=[pltpu.VMEM((ROWBLK, T, T), BF)],
            moved=4 << 20,
        )(plan, *row)

    def spread(ru, rd, fu, fd):
        far = along_y(ru, 1), along_y(rd, -1)
        fu, fd = call(
            relay_kernel, (blocks(FIN), blocks(FIN)), [SMEM] + [VMEM] * 4, moved=3 << 20
        )(plan, *far, fu, fd)
        return (along_y(fu, 1), along_y(fd, -1)), fu

    def hop_back(behind, ahead, *earlier):
        return along_y(after(behind, *earlier), -1), along_y(after(ahead, *earlier), 1)

    def relay_back(got_up, got_down, *earlier):
        to_down, to_up = call(
            return_kernel, (blocks(REL), blocks(REL)), [SMEM, VMEM, VMEM], moved=2 << 20
        )(plan, after(got_up, *earlier), got_down)
        return (along_y(to_down, -1), along_y(to_up, 1)), to_down

    def add_up(local, got_up, got_down, far_up, far_down):
        return call(
            total_kernel,
            (blocks(NB),) * NZ,
            [SMEM] + [VMEM] * 5,
            scratch=[pltpu.VMEM((ROWBLK, T, T), F32)],
            moved=5 << 20,
        )(plan, local, got_up, got_down, far_up, far_down)

    def ring_start(parts, plus, minus):
        return [(parts, 1, plus, along_z(parts[plus], 1))] + [
            (parts, -1, minus, along_z(parts[NZ - minus], -1))
        ]

    def ring_next(rings):
        sums = [
            (moving.astype(F32) + parts[step * (left - 1) % NZ].astype(F32)).astype(BF)
            for parts, step, left, moving in rings
        ]
        return [
            (parts, step, left - 1, along_z(x, step))
            for (parts, step, left, _), x in zip(rings, sums)
        ]

    def ring_end(grad, rings):
        while any(left > 1 for _, _, left, _ in rings):
            more = [r for r in rings if r[2] > 1]
            rings = [r for r in rings if r[2] == 1] + ring_next(more)
        out = grad + rings[0][0][0].astype(F32) + sum(r[3].astype(F32) for r in rings)
        return out.reshape(NB * T, T)

    scratch = [
        pltpu.VMEM((NB + 2, T, T), F32),
        pltpu.VMEM((GLOBALS, T, T), F32),
        pltpu.VMEM((2 * FIN + REQ, T, T), BF),
        pltpu.VMEM((NB, 8 * T, T), F32),
        pltpu.SemaphoreType.DMA((NB,)),
    ]
    full = pltpu.VMEM((ROWBLK + 2 * FIN, T, T), BF)
    every = NB + 2 + RAND + GLOBALS
    grads = (blocks(NB, F32), blocks(FIN), blocks(FIN), blocks(REQ))
    anywhere = pl.BlockSpec(memory_space=pl.ANY)

    krow = [keys.reshape(NB, T, T)] + [None] * (NZ - 1)
    vrow = [values.reshape(NB, T, T)] + [None] * (NZ - 1)

    def step(row, s, *earlier, plus=True, minus=True):
        up, down = row[(NZ + 1 - s) % NZ], row[s - 1]
        if plus:
            row[NZ - s] = along_z(after(up, *earlier) if earlier else up, 1)
        if minus:
            row[s] = along_z(after(down, *earlier) if earlier else down, -1)

    step(krow, 1)
    step(vrow, 1)
    step(krow, 2)
    step(vrow, 2)
    step(krow, 3, plan, vrow[7], vrow[1])
    step(vrow, 3)
    step(krow, 4, minus=False)
    step(vrow, 4, plus=False)
    kpack = pack(krow)
    vpack = pack(vrow)
    kfin, _ = spread(*kpack)
    vfin, vready = spread(*vpack)

    probs, kall, gv, *vback = call(
        probs_kernel,
        (jax.ShapeDtypeStruct((NB, 8 * T, T), F32), blocks(every)) + grads,
        [SMEM] + [VMEM] * (2 + NZ + 2),
        outs_at=[anywhere] + [VMEM] * 5,
        scratch=[full] + scratch,
        flops=2 * 2 * 64 * T**3,
        moved=12 << 20,
        limit=48,
    )(plan, after(q, vready), upstream, *krow, *kfin)
    ds, gk, *kback = call(
        scores_kernel,
        (jax.ShapeDtypeStruct((NB, 8 * T, T), BF),) + grads,
        [SMEM] + [VMEM] * 2 + [anywhere] + [VMEM] * (NZ + 2),
        outs_at=[anywhere] + [VMEM] * 4,
        scratch=[full, pltpu.VMEM((every, T, T), BF)]
        + scratch[:-1]
        + [pltpu.VMEM((NB, 8 * T, T), BF)]
        + [scratch[-1]] * 2,
        flops=2 * 3 * 64 * T**3,
        moved=12 << 20,
        limit=48,
    )(plan, q, upstream, probs, *vrow, *vfin)

    vgot = hop_back(*vback[:2])
    vfar, vsent = relay_back(*vgot, kback[0])
    kgot = hop_back(*kback[:2], vsent)
    dq = call(
        queries_kernel, blocks(NB, F32), [VMEM, VMEM], flops=2 * 64 * T**3, moved=4 << 20
    )(after(ds, vsent), kall)
    kfar, ksent = relay_back(*kgot, dq)
    vparts = add_up(after(vback[2], ksent), *vgot, *vfar)
    vring = ring_start(vparts, 3, 4)
    kring = ring_start(add_up(kback[2], *kgot, *kfar), 4, 3)
    dv = ring_end(gv, vring)
    dk = ring_end(gk, kring)
    return dq.reshape(NB * T, T), dk, dv


def solution(mesh):
    return jax.shard_map(
        per_device,
        mesh=mesh,
        in_specs=(P("seq", "head"),) * 4 + (P("head", None), P(), P()),
        out_specs=(P("seq", "head"),) * 3,
        check_vma=False,
    )
```
